1024 devices in a mesh: row: 16 (over z_lo, y), col: 64 (over x, z_hi, core).
Axes of the slice: x: 8, y: 8, z: 8 (z_hi: 4, z_lo: 2; z = z_hi * 2 + z_lo), core: 2. Of those that a mesh axis runs over, the one named last changes fastest.
Arguments:
- t_pair: float32 [4, 64, 512, 512], P(None, 'row', 'col'), may hold values from -16 to 16
- w_ovov: float32 [512, 512, 1024], P('col', 'row'), may hold values from -0.03125 to 0.03125
Outputs:
- cycle_residual: float32 [512, 4, 16, 512], P('col', None, None, 'row')
The draws below stay inside these ranges and needn't reach their ends.
All inputs are finite; a program needn't handle non-finite values.
Results may differ from the reference program's by a relative error of at most 0.00007.
Values sent between devices are 32-bit elements; how exact they have to be, the bound alone decides.
No kernel may reach another device: no remote copies, remote signals or barrier semaphores. Data moves between devices by JAX's collectives and lax.ppermute only.
A program may use at most 64 MiB of HBM per device.

```python
import jax
import jax.numpy as jnp
from jax import lax

NOCC = 64
NVIRT = 512
IBLK = 4
JBLK = 16


def raised(values, own_key, source, target, shards_of, factor):
    owner, partner = [(jnp.arange(values.shape[position]) // (values.shape[position] // shards_of)).reshape([-1 if axis == position else 1 for axis in range(values.ndim)]) for position in (source, target)]
    chosen = jax.random.permutation(own_key, shards_of)[partner]
    strong = (owner == chosen) | (owner == (partner + shards_of // 2) % shards_of)
    return jnp.where(strong, factor * values, values)


def block_scale(rng, extent, cuts, least, top_value):
    gain, own = 1.0, jax.random.fold_in(rng, 6)
    for axis_at, blocks in cuts:
        steps = jnp.exp(jax.random.uniform(jax.random.fold_in(own, axis_at), (blocks,), jnp.float32, least / len(cuts), top_value / len(cuts)))
        gain = gain * jnp.repeat(steps, extent[axis_at] // blocks).reshape([-1 if axis == axis_at else 1 for axis in range(len(extent))])
    return gain


def noise(key, dims, spread, bound, shards=(), held_as=jnp.bfloat16):
    values = jax.random.normal(key, dims, jnp.float32) * spread
    if len(shards) > 0:
        values = block_scale(key, dims, shards, -0.22, 0.18) * values
    return jnp.clip(values, min=-bound, max=bound).astype(held_as)


def bell_draw_with(own_key, dims, width, bound, cuts, heavy, kind=jnp.bfloat16):
    array = width * jax.random.normal(own_key, dims, jnp.float32)
    if cuts:
        array = array * block_scale(own_key, dims, cuts, -0.22, 0.18)
    return jnp.clip(raised(array, jax.random.fold_in(own_key, 3), *heavy), -bound, bound).astype(kind)


def setup_inputs(seed: int = 0) -> dict:
    streams_of = jax.random.split(jax.random.key(seed), 3)
    return {
        "t_pair": bell_draw_with(streams_of[0], (IBLK, NOCC, NVIRT, NVIRT), 1.0, 16.0, ((1, 16), (2, 64)), (2, 3, 64, 4.0), jnp.float32),
        "w_ovov": noise(streams_of[1], (NVIRT, NVIRT, NOCC * JBLK), (NOCC * NVIRT) ** -0.5, 0.03125, ((0, 64), (1, 16)), jnp.float32),
    }


def reference(t_pair, w_ovov):
    left = jnp.transpose(t_pair, (3, 0, 1, 2)).reshape(NVIRT * IBLK, NOCC * NVIRT)
    integrals = jnp.transpose(w_ovov.reshape(NVIRT, NVIRT, NOCC, JBLK), (2, 0, 3, 1))
    right = integrals.reshape(NOCC * NVIRT, JBLK * NVIRT)
    product = jnp.dot(left, right, preferred_element_type=jnp.float32, precision=lax.Precision.HIGHEST)
    return product.reshape(NVIRT, IBLK, JBLK, NVIRT)
```

```python
import functools

import jax
import jax.numpy as jnp
import numpy as np
from jax import lax
from jax.experimental import pallas as pl
from jax.experimental.pallas import tpu as pltpu
from jax.sharding import PartitionSpec as P

X, ZH, CORES = 8, 4, 2
ZL, Y = 2, 8
GX = 4
XH = X // GX
MEMBERS = GX * CORES
PEERS = XH * ZH
F32 = jnp.float32
BF16 = jnp.bfloat16


def col_of(x, zh, core):
    return (x * ZH + zh) * CORES + core


def col_perm(move):
    pairs = []
    for x in range(X):
        for zh in range(ZH):
            for core in range(CORES):
                pairs.append((col_of(x, zh, core), col_of(*move(x, zh, core))))
    return pairs


def row_perm(move):
    pairs = []
    for zl in range(ZL):
        for y in range(Y):
            z2, y2 = move(zl, y)
            pairs.append((zl * Y + y, z2 * Y + y2 % Y))
    return pairs


MEMBER_GROUPS = [
    [col_of(xh * GX + xl, zh, core) for xl in range(GX) for core in range(CORES)]
    for xh in range(XH)
    for zh in range(ZH)
]
PEER_GROUPS = [
    [col_of(xh * GX + xl, zh, core) for xh in range(XH) for zh in range(ZH)]
    for xl in range(GX)
    for core in range(CORES)
]


BLOCKS = [((0, 1), 0)]
for _step in range(1, Y // 2):
    BLOCKS += [((0, 1), -_step), ((0, 1), _step)]
BLOCKS += [((0,), Y // 2), ((1,), Y // 2)]


def row_table():
    table = np.zeros((ZL * Y, len(BLOCKS) * ZL), np.int32)
    for zl in range(ZL):
        for y in range(Y):
            for n, (which, shift) in enumerate(BLOCKS):
                for at in range(ZL):
                    z = zl ^ which[min(at, len(which) - 1)]
                    table[zl * Y + y, n * ZL + at] = z * Y + (y + shift) % Y
    return table


def col_table():
    table = np.zeros((X * ZH * CORES, MEMBERS), np.int32)
    for col in range(table.shape[0]):
        x, core = col // (ZH * CORES), col % CORES
        for n in range(MEMBERS):
            source = (x - n % GX) % GX
            table[col, n] = source * CORES + (core if n < GX else 1 - core)
    return table


def split2(v):
    hi = v.astype(BF16)
    return hi, (v - hi.astype(F32)).astype(BF16)


def regroup_kernel(t_ref, out_ref):
    blocks, rows, virt = t_ref.shape[0], t_ref.shape[1], t_ref.shape[2]
    run = virt // (X * ZH * CORES)
    src = lax.broadcasted_iota(jnp.int32, (virt, virt), 0)
    dst = lax.broadcasted_iota(jnp.int32, (virt, virt), 1)
    r = dst % run
    zh = (dst // run) % ZH
    xh = (dst // (run * ZH)) % XH
    core = (dst // (run * ZH * XH)) % CORES
    xl = dst // (run * ZH * XH * CORES)
    want = ((((xh * GX + xl) * ZH + zh) * CORES) + core) * run + r
    onehot = jnp.where(src == want, 1.0, 0.0).astype(BF16)
    width = virt // MEMBERS
    for i in range(blocks):
        v = t_ref[i]
        hi = v.astype(BF16)
        rest = v - hi.astype(F32)
        mid = rest.astype(BF16)
        low = (rest - mid.astype(F32)).astype(BF16)
        parts = jnp.dot(
            jnp.concatenate([hi, mid, low], axis=0), onehot, preferred_element_type=F32
        )
        moved = (parts[:rows] + parts[rows : 2 * rows]) + parts[2 * rows :]
        for m in range(MEMBERS):
            out_ref[m, :, i * width : (i + 1) * width] = moved[:, m * width : (m + 1) * width]


def regroup(t):
    blocks, ks, cs, virt = t.shape
    rows = ks * cs
    return pl.pallas_call(
        regroup_kernel,
        out_shape=jax.ShapeDtypeStruct((MEMBERS, rows, blocks * virt // MEMBERS), F32),
        cost_estimate=pl.CostEstimate(flops=6 * blocks * rows * virt * virt, bytes_accessed=t.size * 8, transcendentals=0),
    )(t.reshape(blocks, rows, virt))


def multiply_kernel(has_acc, blocks, *refs):
    s_ref, t_ref = refs[0], refs[1]
    w_refs = refs[2 : 2 + MEMBERS]
    out_ref = refs[-1]

    @pl.when(pl.program_id(0) == 0)
    def _():
        if has_acc:
            out_ref[...] = refs[2 + MEMBERS][...]
        else:
            out_ref[...] = jnp.zeros_like(out_ref)

    left = jnp.concatenate([t_ref[0, s_ref[len(BLOCKS) * ZL + n]] for n in range(MEMBERS)], axis=0)
    right = jnp.concatenate([w[0] for w in w_refs], axis=0)
    lh, ll = split2(left)
    rh, rl = split2(right)
    dims = (((0,), (0,)), ((), ()))
    total = lax.dot_general(
        jnp.concatenate([lh, lh, ll], axis=0),
        jnp.concatenate([rh, rl, rh], axis=0),
        dims,
        preferred_element_type=F32,
    )
    run = total.shape[0] // (blocks * PEERS)
    total = total.reshape(blocks, PEERS, run, total.shape[1])
    for i in range(blocks):
        out_ref[:, i * run : (i + 1) * run, :] += total[i]


def multiply(scalars, at, t, ws, acc, blocks):
    rows, width = t.shape[2], t.shape[3]
    wide = ws[0].shape[2]
    out_shape = (PEERS, width // PEERS, wide)
    in_specs = [pl.BlockSpec((1, MEMBERS, rows, width), lambda z, s: (z, 0, 0, 0))]
    in_specs += [pl.BlockSpec((1, rows, wide), lambda z, s: (s[at * ZL + z], 0, 0))] * MEMBERS
    args = [scalars, t, *ws]
    whole = pl.BlockSpec(out_shape, lambda z, s: (0, 0, 0))
    aliases = {}
    if acc is not None:
        in_specs.append(whole)
        args.append(acc)
        aliases = {len(args) - 1: 0}
    return pl.pallas_call(
        functools.partial(multiply_kernel, acc is not None, blocks),
        grid_spec=pltpu.PrefetchScalarGridSpec(
            num_scalar_prefetch=1, grid=(t.shape[0],), in_specs=in_specs, out_specs=whole
        ),
        out_shape=jax.ShapeDtypeStruct(out_shape, F32),
        input_output_aliases=aliases,
        cost_estimate=pl.CostEstimate(
            flops=6 * t.shape[0] * MEMBERS * rows * width * wide, bytes_accessed=t.size * 4 + 2 * len(ws) * rows * wide * 4, transcendentals=0
        ),
    )(*args)


def shards(t_pair, w_ovov):
    blocks, ks, cs, virt = t_pair.shape
    rows = ks * cs
    row, col = lax.axis_index("row"), lax.axis_index("col")
    scalars = jnp.concatenate(
        [
            lax.dynamic_index_in_dim(jnp.asarray(row_table()), row, keepdims=False),
            lax.dynamic_index_in_dim(jnp.asarray(col_table()), col, keepdims=False),
        ]
    )

    sent = regroup(t_pair)
    mine = lax.all_to_all(sent, "col", 0, 0, tiled=True, axis_index_groups=MEMBER_GROUPS)

    depth, wb, kj = w_ovov.shape
    occupied = ks * ZL * Y
    pairs = kj // occupied
    own_w = w_ovov.reshape(cs, wb, occupied, pairs).transpose(2, 0, 3, 1).reshape(ZL * Y, rows, pairs * wb)
    swap_core = col_perm(lambda x, zh, c: (x, zh, 1 - c))
    near = [own_w]
    for s in range(1, GX):
        near.append(
            lax.ppermute(own_w, "col", col_perm(lambda x, zh, c, s=s: ((x // GX) * GX + (x + s) % GX, zh, c)))
        )
    far = [lax.ppermute(w, "col", swap_core) for w in near]
    ws = near + far
    other = lax.ppermute(mine, "row", row_perm(lambda z, q: (1 - z, q)))
    own = jnp.stack([mine, other])
    up_perm = row_perm(lambda z, q: (z, q + 1))
    down_perm = row_perm(lambda z, q: (z, q - 1))
    got = [own]
    up = down = own
    for _ in range(1, Y // 2):
        up = lax.ppermute(up, "row", up_perm)
        down = lax.ppermute(down, "row", down_perm)
        got += [up, down]
    got.append(lax.ppermute(up[:1], "row", up_perm))
    got.append(lax.ppermute(down[1:], "row", down_perm))

    acc = None
    for at, block in enumerate(got):
        acc = multiply(scalars, at, block, ws, acc, blocks)

    arrived = lax.all_to_all(acc, "col", 0, 0, tiled=True, axis_index_groups=PEER_GROUPS)
    total = jnp.sum(arrived, axis=0)
    run = virt // (X * ZH * CORES)
    return total.reshape(blocks, run, pairs, wb).transpose(1, 0, 2, 3)


def solution(mesh):
    return jax.shard_map(
        shards,
        mesh=mesh,
        in_specs=(P(None, "row", "col", None), P("col", "row", None)),
        out_specs=P("col", None, None, "row"),
        check_vma=False,
    )
```

```python
import functools

import jax
import jax.numpy as jnp
import numpy as np
from jax import lax
from jax.experimental import pallas as pl
from jax.experimental.pallas import tpu as pltpu
from jax.sharding import PartitionSpec as P

X, ZH, CORES = 8, 4, 2
ZL, Y = 2, 8
GX = 2
XH = X // GX
MEMBERS = GX * CORES
PEERS = XH * ZH
F32 = jnp.float32
BF16 = jnp.bfloat16


def col_of(x, zh, core):
    return (x * ZH + zh) * CORES + core


def col_perm(move):
    pairs = []
    for x in range(X):
        for zh in range(ZH):
            for core in range(CORES):
                pairs.append((col_of(x, zh, core), col_of(*move(x, zh, core))))
    return pairs


def row_perm(move):
    pairs = []
    for zl in range(ZL):
        for y in range(Y):
            z2, y2 = move(zl, y)
            pairs.append((zl * Y + y, z2 * Y + y2 % Y))
    return pairs


MEMBER_GROUPS = [
    [
        (zl * Y + y) * (X * ZH * CORES) + col_of(xh * GX + xl, zh, core)
        for zl in range(ZL)
        for xl in range(GX)
        for core in range(CORES)
    ]
    for y in range(Y)
    for xh in range(XH)
    for zh in range(ZH)
]
PEER_GROUPS = [
    [col_of(xh * GX + xl, zh, core) for xh in range(XH) for zh in range(ZH)]
    for xl in range(GX)
    for core in range(CORES)
]


CALLS = [[((0, 1), 0)]]
for _step in range(1, Y // 2):
    CALLS.append([((0, 1), -_step), ((0, 1), _step)])
CALLS.append([((0,), Y // 2), ((1,), Y // 2)])
PLACES = [[(zl, shift) for which, shift in call for zl in which] for call in CALLS]
SLOTS = sum(len(places) for places in PLACES)


def row_table():
    table = np.zeros((ZL * Y, SLOTS), np.int32)
    for row in range(ZL * Y):
        table[row] = [zl * Y + (row + shift) % Y for places in PLACES for zl, shift in places]
    return table


def col_table():
    table = np.zeros((X * ZH * CORES, MEMBERS), np.int32)
    for col in range(table.shape[0]):
        x, core = col // (ZH * CORES), col % CORES
        for n in range(MEMBERS):
            source = (x - n % GX) % GX
            table[col, n] = source * CORES + (core if n < GX else 1 - core)
    return table


def split2(v):
    hi = v.astype(BF16)
    return hi, (v - hi.astype(F32)).astype(BF16)


def regroup_kernel(t_ref, out_ref):
    blocks, rows, virt = t_ref.shape[0], t_ref.shape[1], t_ref.shape[2]
    run = virt // (X * ZH * CORES)
    src = lax.broadcasted_iota(jnp.int32, (virt, virt), 0)
    dst = lax.broadcasted_iota(jnp.int32, (virt, virt), 1)
    r = dst % run
    zh = (dst // run) % ZH
    xh = (dst // (run * ZH)) % XH
    core = (dst // (run * ZH * XH)) % CORES
    xl = dst // (run * ZH * XH * CORES)
    want = ((((xh * GX + xl) * ZH + zh) * CORES) + core) * run + r
    onehot = jnp.where(src == want, 1.0, 0.0).astype(BF16)
    width = virt // MEMBERS
    for i in range(blocks):
        v = t_ref[i]
        hi = v.astype(BF16)
        rest = v - hi.astype(F32)
        mid = rest.astype(BF16)
        low = (rest - mid.astype(F32)).astype(BF16)
        parts = jnp.dot(
            jnp.concatenate([hi, mid, low], axis=0), onehot, preferred_element_type=F32
        )
        moved = (parts[:rows] + parts[rows : 2 * rows]) + parts[2 * rows :]
        for m in range(MEMBERS):
            out_ref[m, :, i * width : (i + 1) * width] = moved[:, m * width : (m + 1) * width]


def regroup(t):
    blocks, ks, cs, virt = t.shape
    rows = ks * cs
    return pl.pallas_call(
        regroup_kernel,
        out_shape=jax.ShapeDtypeStruct((MEMBERS, rows, blocks * virt // MEMBERS), F32),
        cost_estimate=pl.CostEstimate(flops=6 * blocks * rows * virt * virt, bytes_accessed=t.size * 8, transcendentals=0),
    )(t.reshape(blocks, rows, virt))


def multiply_kernel(has_acc, blocks, order_at, n_t, n_w, *refs):
    s_ref = refs[0]
    t_refs = refs[1 : 1 + n_t]
    w_refs = refs[1 + n_t : 1 + n_t + n_w]
    out_ref = refs[-1]
    left = jnp.concatenate(
        [t[z, s_ref[order_at + n]] for t in t_refs for z in range(t.shape[0]) for n in range(MEMBERS)], axis=0
    )
    right = jnp.concatenate([w[0] for w in w_refs], axis=0)
    lh, ll = split2(left)
    rh, rl = split2(right)
    total = lax.dot_general(
        jnp.concatenate([lh, lh, ll], axis=0),
        jnp.concatenate([rh, rl, rh], axis=0),
        (((0,), (0,)), ((), ())),
        preferred_element_type=F32,
    )
    run = total.shape[0] // (blocks * PEERS)
    total = total.reshape(blocks, PEERS, run, total.shape[1])
    for i in range(blocks):
        rows = slice(i * run, (i + 1) * run)
        if has_acc:
            out_ref[:, rows, :] = refs[1 + n_t + n_w][:, rows, :] + total[i]
        else:
            out_ref[:, rows, :] = total[i]


def multiply(scalars, at, ts, ws, acc, blocks):
    rows, width = ts[0].shape[2], ts[0].shape[3]
    wide = ws[0].shape[2]
    out_shape = (PEERS, width // PEERS, wide)
    first = sum(len(places) for places in PLACES[:at])
    slots = range(first, first + len(PLACES[at]))
    in_specs = [pl.BlockSpec(t.shape, lambda z, s: (0, 0, 0, 0)) for t in ts]
    in_specs += [
        pl.BlockSpec((1, rows, wide), lambda z, s, slot=slot: (s[slot], 0, 0)) for slot in slots for _ in ws
    ]
    args = [scalars, *ts, *(list(ws) * len(slots))]
    whole = pl.BlockSpec(out_shape, lambda z, s: (0, 0, 0))
    if acc is not None:
        in_specs.append(whole)
        args.append(acc)
    depth = len(slots) * len(ws) * rows
    return pl.pallas_call(
        functools.partial(multiply_kernel, acc is not None, blocks, SLOTS, len(ts), len(slots) * len(ws)),
        grid_spec=pltpu.PrefetchScalarGridSpec(num_scalar_prefetch=1, grid=(1,), in_specs=in_specs, out_specs=whole),
        out_shape=jax.ShapeDtypeStruct(out_shape, F32),
        compiler_params=pltpu.CompilerParams(vmem_limit_bytes=32 * 2**20),
        cost_estimate=pl.CostEstimate(
            flops=6 * depth * width * wide, bytes_accessed=4 * depth * (width + wide), transcendentals=0
        ),
    )(*args)


def shards(t_pair, w_ovov):
    blocks, ks, cs, virt = t_pair.shape
    rows = ks * cs
    row, col = lax.axis_index("row"), lax.axis_index("col")
    scalars = jnp.concatenate(
        [
            lax.dynamic_index_in_dim(jnp.asarray(row_table()), row, keepdims=False),
            lax.dynamic_index_in_dim(jnp.asarray(col_table()), col, keepdims=False),
        ]
    )

    sent = regroup(t_pair)
    own = lax.all_to_all(
        jnp.concatenate([sent] * ZL), ("row", "col"), 0, 0, tiled=True, axis_index_groups=MEMBER_GROUPS
    ).reshape(ZL, MEMBERS, rows, -1)

    depth, wb, kj = w_ovov.shape
    occupied = ks * ZL * Y
    pairs = kj // occupied
    own_w = w_ovov.reshape(cs, wb, occupied, pairs).transpose(2, 0, 3, 1).reshape(ZL * Y, rows, pairs * wb)
    swap_core = col_perm(lambda x, zh, c: (x, zh, 1 - c))
    swap_x = col_perm(lambda x, zh, c: (x ^ 1, zh, c))
    w_x = lax.ppermute(own_w, "col", swap_x)
    w_c = lax.ppermute(own_w, "col", swap_core)

    up_perm = row_perm(lambda z, q: (z, q + 1))
    down_perm = row_perm(lambda z, q: (z, q - 1))
    got = [(own,)]
    up = down = own
    for step in range(1, Y // 2):
        up = lax.ppermute(up, "row", up_perm)
        down = lax.ppermute(down, "row", down_perm)
        got.append((up, down))
        if step == 2:
            up, down, w_x, w_c = lax.optimization_barrier((up, down, w_x, w_c))
    w_xc = lax.ppermute(w_x, "col", swap_core)
    got.append((lax.ppermute(up[:1], "row", up_perm), lax.ppermute(down[1:], "row", down_perm)))
    ws = [own_w, w_x, w_c, w_xc]

    acc = None
    for at, ts in enumerate(got):
        acc = multiply(scalars, at, ts, ws, acc, blocks)

    arrived = lax.all_to_all(acc, "col", 0, 0, tiled=True, axis_index_groups=PEER_GROUPS)
    total = jnp.sum(arrived, axis=0)
    run = virt // (X * ZH * CORES)
    return total.reshape(blocks, run, pairs, wb).transpose(1, 0, 2, 3)


def solution(mesh):
    return jax.shard_map(
        shards,
        mesh=mesh,
        in_specs=(P(None, "row", "col", None), P("col", "row", None)),
        out_specs=P("col", None, None, "row"),
        check_vma=False,
    )
```

```python
import functools

import jax
import jax.numpy as jnp
import numpy as np
from jax import lax
from jax.experimental import pallas as pl
from jax.experimental.pallas import tpu as pltpu
from jax.sharding import PartitionSpec as P

X, ZH, CORES = 8, 4, 2
ZL, Y = 2, 8
GX = 2
XH = X // GX
MEMBERS = GX * CORES
PEERS = XH * ZH
F32 = jnp.float32
BF16 = jnp.bfloat16


def col_of(x, zh, core):
    return (x * ZH + zh) * CORES + core


def col_perm(move):
    pairs = []
    for x in range(X):
        for zh in range(ZH):
            for core in range(CORES):
                pairs.append((col_of(x, zh, core), col_of(*move(x, zh, core))))
    return pairs


def row_perm(move):
    pairs = []
    for zl in range(ZL):
        for y in range(Y):
            z2, y2 = move(zl, y)
            pairs.append((zl * Y + y, z2 * Y + y2 % Y))
    return pairs


MEMBER_GROUPS = [
    [
        (zl * Y + y) * (X * ZH * CORES) + col_of(xh * GX + xl, zh, core)
        for zl in range(ZL)
        for xl in range(GX)
        for core in range(CORES)
    ]
    for y in range(Y)
    for xh in range(XH)
    for zh in range(ZH)
]
PEER_GROUPS = [
    [col_of(xh * GX + xl, zh, core) for xh in range(XH) for zh in range(ZH)]
    for xl in range(GX)
    for core in range(CORES)
]


def low_pair(y):
    return y ^ 1


def high_pair(y):
    return (y + 1 if y % 2 else y - 1) % Y


MEETS = [(low_pair, high_pair), (high_pair, low_pair)]


def sources(y):
    per_half = []
    for first, second in MEETS:
        steps = [[lambda q: q], [first]]
        held = steps[0] + steps[1]
        for n in range(2, Y // 2 + 1):
            meet = second if n % 2 == 0 else first
            held = [lambda q, f=f, meet=meet: f(meet(q)) for f in held]
            steps.append(held)
        per_half.append([[f(y) for f in step] for step in steps])
    zero, one = per_half
    calls = [[(0, y), (1, y)] + [(0, q) for q in zero[1]] + [(1, q) for q in one[1]]]
    for n in range(2, Y // 2 + 1):
        calls.append([(0, q) for q in zero[n]] + [(1, q) for q in one[n]])
    return calls


COUNTS = [len(call) for call in sources(0)]
SLOTS = sum(COUNTS)


def row_table():
    table = np.zeros((ZL * Y, SLOTS), np.int32)
    for row in range(ZL * Y):
        table[row] = [zl * Y + q for call in sources(row % Y) for zl, q in call]
    return table


def col_table():
    table = np.zeros((X * ZH * CORES, MEMBERS), np.int32)
    for col in range(table.shape[0]):
        x, core = col // (ZH * CORES), col % CORES
        for n in range(MEMBERS):
            source = (x - n % GX) % GX
            table[col, n] = source * CORES + (core if n < GX else 1 - core)
    return table


def split2(v):
    hi = v.astype(BF16)
    return hi, (v - hi.astype(F32)).astype(BF16)


def regroup_kernel(t_ref, out_ref):
    blocks, rows, virt = t_ref.shape[0], t_ref.shape[1], t_ref.shape[2]
    run = virt // (X * ZH * CORES)
    src = lax.broadcasted_iota(jnp.int32, (virt, virt), 0)
    dst = lax.broadcasted_iota(jnp.int32, (virt, virt), 1)
    r = dst % run
    zh = (dst // run) % ZH
    xh = (dst // (run * ZH)) % XH
    core = (dst // (run * ZH * XH)) % CORES
    xl = dst // (run * ZH * XH * CORES)
    want = ((((xh * GX + xl) * ZH + zh) * CORES) + core) * run + r
    onehot = jnp.where(src == want, 1.0, 0.0).astype(BF16)
    width = virt // MEMBERS
    for i in range(blocks):
        v = t_ref[i]
        hi = v.astype(BF16)
        rest = v - hi.astype(F32)
        mid = rest.astype(BF16)
        low = (rest - mid.astype(F32)).astype(BF16)
        parts = jnp.dot(
            jnp.concatenate([hi, mid, low], axis=0), onehot, preferred_element_type=F32
        )
        moved = (parts[:rows] + parts[rows : 2 * rows]) + parts[2 * rows :]
        for m in range(MEMBERS):
            piece = moved[:, m * width : (m + 1) * width]
            for z in range(ZL):
                out_ref[z * MEMBERS + m, :, i * width : (i + 1) * width] = piece


def regroup(t):
    blocks, ks, cs, virt = t.shape
    rows = ks * cs
    return pl.pallas_call(
        regroup_kernel,
        out_shape=jax.ShapeDtypeStruct((ZL * MEMBERS, rows, blocks * virt // MEMBERS), F32),
        cost_estimate=pl.CostEstimate(flops=6 * blocks * rows * virt * virt, bytes_accessed=t.size * 8, transcendentals=0),
    )(t.reshape(blocks, rows, virt))


def multiply_kernel(has_acc, blocks, order_at, n_t, n_w, *refs):
    s_ref = refs[0]
    t_refs = refs[1 : 1 + n_t]
    w_refs = refs[1 + n_t : 1 + n_t + n_w]
    out_ref = refs[-1]
    left = jnp.concatenate(
        [t[z, s_ref[order_at + n]] for t in t_refs for z in range(t.shape[0]) for n in range(MEMBERS)], axis=0
    )
    right = jnp.concatenate([w[0] for w in w_refs], axis=0)
    lh, ll = split2(left)
    rh, rl = split2(right)
    total = lax.dot_general(
        jnp.concatenate([lh, lh, ll], axis=0),
        jnp.concatenate([rh, rl, rh], axis=0),
        (((0,), (0,)), ((), ())),
        preferred_element_type=F32,
    )
    run = total.shape[0] // (blocks * PEERS)
    total = total.reshape(blocks, PEERS, run, total.shape[1])
    for i in range(blocks):
        rows = slice(i * run, (i + 1) * run)
        if has_acc:
            out_ref[:, rows, :] = refs[1 + n_t + n_w][:, rows, :] + total[i]
        else:
            out_ref[:, rows, :] = total[i]


def multiply(scalars, at, ts, ws, acc, blocks):
    rows, width = ts[0].shape[2], ts[0].shape[3]
    wide = ws[0].shape[2]
    out_shape = (PEERS, width // PEERS, wide)
    first = sum(COUNTS[:at])
    slots = range(first, first + COUNTS[at])
    in_specs = [pl.BlockSpec(t.shape, lambda z, s: (0, 0, 0, 0)) for t in ts]
    in_specs += [
        pl.BlockSpec((1, rows, wide), lambda z, s, slot=slot: (s[slot], 0, 0)) for slot in slots for _ in ws
    ]
    args = [scalars, *ts, *(list(ws) * len(slots))]
    whole = pl.BlockSpec(out_shape, lambda z, s: (0, 0, 0))
    if acc is not None:
        in_specs.append(whole)
        args.append(acc)
    depth = len(slots) * len(ws) * rows
    return pl.pallas_call(
        functools.partial(multiply_kernel, acc is not None, blocks, SLOTS, len(ts), len(slots) * len(ws)),
        grid_spec=pltpu.PrefetchScalarGridSpec(num_scalar_prefetch=1, grid=(1,), in_specs=in_specs, out_specs=whole),
        out_shape=jax.ShapeDtypeStruct(out_shape, F32),
        compiler_params=pltpu.CompilerParams(vmem_limit_bytes=32 * 2**20),
        cost_estimate=pl.CostEstimate(
            flops=6 * depth * width * wide, bytes_accessed=4 * depth * (width + wide), transcendentals=0
        ),
    )(*args)


def shards(t_pair, w_ovov):
    blocks, ks, cs, virt = t_pair.shape
    rows = ks * cs
    row, col = lax.axis_index("row"), lax.axis_index("col")
    scalars = jnp.concatenate(
        [
            lax.dynamic_index_in_dim(jnp.asarray(row_table()), row, keepdims=False),
            lax.dynamic_index_in_dim(jnp.asarray(col_table()), col, keepdims=False),
        ]
    )

    sent = regroup(t_pair)
    own = lax.all_to_all(
        sent, ("row", "col"), 0, 0, tiled=True, axis_index_groups=MEMBER_GROUPS
    ).reshape(ZL, MEMBERS, rows, -1)

    depth, wb, kj = w_ovov.shape
    occupied = ks * ZL * Y
    pairs = kj // occupied
    own_w = w_ovov.reshape(cs, wb, occupied, pairs).transpose(2, 0, 3, 1).reshape(ZL * Y, rows, pairs * wb)
    swap_core = col_perm(lambda x, zh, c: (x, zh, 1 - c))
    swap_x = col_perm(lambda x, zh, c: (x ^ 1, zh, c))
    w_x = lax.ppermute(own_w, "col", swap_x)
    w_c = lax.ppermute(own_w, "col", swap_core)

    meets = [[row_perm(lambda z, q, f=f: (z, f(q))) for f in pair] for pair in MEETS]
    halves = [own[:1], own[1:]]
    got = [(own,)]
    for step in range(1, Y // 2 + 1):
        moved = [lax.ppermute(h, "row", meets[n][(step + 1) % 2]) for n, h in enumerate(halves)]
        if step == 1:
            got[0] += tuple(moved)
            halves = [jnp.concatenate([h, m]) for h, m in zip(halves, moved)]
        else:
            got.append(tuple(moved))
            halves = moved
        if step == 2:
            *halves, w_x, w_c = lax.optimization_barrier((*halves, w_x, w_c))
            got[-1] = tuple(halves)
    w_xc = lax.ppermute(w_x, "col", swap_core)
    ws = [own_w, w_x, w_c, w_xc]

    acc = None
    for at, ts in enumerate(got):
        acc = multiply(scalars, at, ts, ws, acc, blocks)

    arrived = lax.all_to_all(acc, "col", 0, 0, tiled=True, axis_index_groups=PEER_GROUPS)
    total = jnp.sum(arrived, axis=0)
    run = virt // (X * ZH * CORES)
    return total.reshape(blocks, run, pairs, wb).transpose(1, 0, 2, 3)


def solution(mesh):
    return jax.shard_map(
        shards,
        mesh=mesh,
        in_specs=(P(None, "row", "col", None), P("col", "row", None)),
        out_specs=P("col", None, None, "row"),
        check_vma=False,
    )
```

```python
import functools

import jax
import jax.numpy as jnp
import numpy as np
from jax import lax
from jax.experimental import pallas as pl
from jax.experimental.pallas import tpu as pltpu
from jax.sharding import PartitionSpec as P

X, ZH, CORES = 8, 4, 2
ZL, Y = 2, 8
GX, GZ = 1, 2
XH, ZG = X // GX, ZH // GZ
MEMBERS = GX * GZ * CORES
PEERS = XH * ZG
F32 = jnp.float32
BF16 = jnp.bfloat16


def col_of(x, zh, core):
    return (x * ZH + zh) * CORES + core


def col_perm(move):
    pairs = []
    for x in range(X):
        for zh in range(ZH):
            for core in range(CORES):
                pairs.append((col_of(x, zh, core), col_of(*move(x, zh, core))))
    return pairs


def row_perm(move):
    pairs = []
    for zl in range(ZL):
        for y in range(Y):
            z2, y2 = move(zl, y)
            pairs.append((zl * Y + y, z2 * Y + y2 % Y))
    return pairs


GROUP = [(xl, zm, core) for xl in range(GX) for zm in range(GZ) for core in range(CORES)]
BASES = [(xh * GX, zg * GZ) for xh in range(XH) for zg in range(ZG)]
MEMBER_GROUPS = [
    [(zl * Y + y) * (X * ZH * CORES) + col_of(x + xl, zh + zm, core) for zl in range(ZL) for xl, zm, core in GROUP]
    for y in range(Y)
    for x, zh in BASES
]
PEER_GROUPS = [[col_of(x + xl, zh + zm, core) for x, zh in BASES] for xl, zm, core in GROUP]
NEAR = [(dx, dz) for dx in range(GX) for dz in range(GZ)]
FROM = [(dx, dz, dc) for dc in range(CORES) for dx, dz in NEAR]


def low_pair(y):
    return y ^ 1


def high_pair(y):
    return (y + 1 if y % 2 else y - 1) % Y


MEETS = [(low_pair, high_pair), (high_pair, low_pair)]


def sources(y):
    per_half = []
    for first, second in MEETS:
        steps = [[lambda q: q], [first]]
        held = steps[0] + steps[1]
        for n in range(2, Y // 2 + 1):
            meet = second if n % 2 == 0 else first
            held = [lambda q, f=f, meet=meet: f(meet(q)) for f in held]
            steps.append(held)
        per_half.append([[f(y) for f in step] for step in steps])
    zero, one = per_half
    calls = [[(0, y), (1, y)] + [(0, q) for q in zero[1]] + [(1, q) for q in one[1]]]
    for n in range(2, Y // 2 + 1):
        calls.append([(0, q) for q in zero[n]] + [(1, q) for q in one[n]])
    return calls


COUNTS = [len(call) for call in sources(0)]
SLOTS = sum(COUNTS)


HOLD = 3
EVERY = list(range(MEMBERS))
LATE = [n for n, (dx, dz, dc) in enumerate(FROM) if dx + dz == 2]
EARLY = [n for n in EVERY if n not in LATE]
if LATE:
    PLAN = [((0,), EARLY), ((1,), EARLY), ((2,), EARLY), ((0, 1, 2), LATE), ((3,), EVERY)]
else:
    PLAN = [((n,), EVERY) for n in range(len(COUNTS))]


def row_table():
    table = np.zeros((ZL * Y, SLOTS), np.int32)
    for row in range(ZL * Y):
        table[row] = [zl * Y + q for call in sources(row % Y) for zl, q in call]
    return table


def col_table():
    table = np.zeros((X * ZH * CORES, MEMBERS), np.int32)
    for col in range(table.shape[0]):
        x, zh, core = col // (ZH * CORES) % GX, col // CORES % GZ, col % CORES
        table[col] = [((x ^ dx) * GZ + (zh ^ dz)) * CORES + (core ^ dc) for dx, dz, dc in FROM]
    return table


def split2(v):
    hi = v.astype(BF16)
    return hi, (v - hi.astype(F32)).astype(BF16)


def regroup_kernel(t_ref, out_ref):
    blocks, rows, virt = t_ref.shape
    run = virt // (X * ZH * CORES)
    src = lax.broadcasted_iota(jnp.int32, (virt, virt), 0)
    dst = lax.broadcasted_iota(jnp.int32, (virt, virt), 1)
    r = dst % run
    zg = (dst // run) % ZG
    xh = (dst // (run * ZG)) % XH
    core = (dst // (run * PEERS)) % CORES
    zm = (dst // (run * PEERS * CORES)) % GZ
    xl = dst // (run * PEERS * CORES * GZ)
    want = (((((xh * GX + xl) * ZG + zg) * GZ + zm) * CORES) + core) * run + r
    onehot = jnp.where(src == want, 1.0, 0.0).astype(BF16)
    width = virt // MEMBERS
    for i in range(blocks):
        v = t_ref[i]
        hi = v.astype(BF16)
        rest = v - hi.astype(F32)
        mid = rest.astype(BF16)
        low = (rest - mid.astype(F32)).astype(BF16)
        parts = jnp.dot(
            jnp.concatenate([hi, mid, low], axis=0), onehot, preferred_element_type=F32
        )
        moved = (parts[:rows] + parts[rows : 2 * rows]) + parts[2 * rows :]
        for m in range(MEMBERS):
            piece = moved[:, m * width : (m + 1) * width]
            for z in range(ZL):
                out_ref[z * MEMBERS + m, :, i * width : (i + 1) * width] = piece


def regroup(t):
    blocks, ks, cs, virt = t.shape
    rows = ks * cs
    return pl.pallas_call(
        regroup_kernel,
        out_shape=jax.ShapeDtypeStruct((ZL * MEMBERS, rows, blocks * virt // MEMBERS), F32),
        cost_estimate=pl.CostEstimate(flops=6 * blocks * rows * virt * virt, bytes_accessed=t.size * 8, transcendentals=0),
    )(t.reshape(blocks, rows, virt))


def multiply_kernel(has_acc, blocks, picks, n_t, n_w, *refs):
    s_ref = refs[0]
    t_refs = refs[1 : 1 + n_t]
    w_refs = refs[1 + n_t : 1 + n_t + n_w]
    out_ref = refs[-1]
    left = jnp.concatenate(
        [t[z, s_ref[SLOTS + n]] for t in t_refs for z in range(t.shape[0]) for n in picks], axis=0
    )
    right = jnp.concatenate([w[0] for w in w_refs], axis=0)
    lh, ll = split2(left)
    rh, rl = split2(right)
    total = lax.dot_general(
        jnp.concatenate([lh, lh, ll], axis=0),
        jnp.concatenate([rh, rl, rh], axis=0),
        (((0,), (0,)), ((), ())),
        preferred_element_type=F32,
    )
    run = total.shape[0] // (blocks * PEERS)
    total = total.reshape(blocks, PEERS, run, total.shape[1])
    for i in range(blocks):
        rows = slice(i * run, (i + 1) * run)
        if has_acc:
            out_ref[:, rows, :] = refs[1 + n_t + n_w][:, rows, :] + total[i]
        else:
            out_ref[:, rows, :] = total[i]


def multiply(scalars, at, ts, ws, picks, acc, blocks):
    ws = [ws[n] for n in picks]
    rows, width = ts[0].shape[2], ts[0].shape[3]
    wide = ws[0].shape[2]
    out_shape = (PEERS, width // PEERS, wide)
    slots = [sum(COUNTS[:n]) + m for n in at for m in range(COUNTS[n])]
    in_specs = [pl.BlockSpec(t.shape, lambda z, s: (0, 0, 0, 0)) for t in ts]
    in_specs += [
        pl.BlockSpec((1, rows, wide), lambda z, s, slot=slot: (s[slot], 0, 0)) for slot in slots for _ in ws
    ]
    args = [scalars, *ts, *(list(ws) * len(slots))]
    whole = pl.BlockSpec(out_shape, lambda z, s: (0, 0, 0))
    if acc is not None:
        in_specs.append(whole)
        args.append(acc)
    depth = len(slots) * len(ws) * rows
    return pl.pallas_call(
        functools.partial(multiply_kernel, acc is not None, blocks, picks, len(ts), len(slots) * len(ws)),
        grid_spec=pltpu.PrefetchScalarGridSpec(num_scalar_prefetch=1, grid=(1,), in_specs=in_specs, out_specs=whole),
        out_shape=jax.ShapeDtypeStruct(out_shape, F32),
        compiler_params=pltpu.CompilerParams(vmem_limit_bytes=32 * 2**20),
        cost_estimate=pl.CostEstimate(
            flops=6 * depth * width * wide, bytes_accessed=4 * depth * (width + wide), transcendentals=0
        ),
    )(*args)


def shards(t_pair, w_ovov):
    blocks, ks, cs, virt = t_pair.shape
    rows = ks * cs
    row, col = lax.axis_index("row"), lax.axis_index("col")
    scalars = jnp.concatenate(
        [
            lax.dynamic_index_in_dim(jnp.asarray(row_table()), row, keepdims=False),
            lax.dynamic_index_in_dim(jnp.asarray(col_table()), col, keepdims=False),
        ]
    )

    sent = regroup(t_pair)
    own = lax.all_to_all(
        sent, ("row", "col"), 0, 0, tiled=True, axis_index_groups=MEMBER_GROUPS
    ).reshape(ZL, MEMBERS, rows, -1)

    depth, wb, kj = w_ovov.shape
    occupied = ks * ZL * Y
    pairs = kj // occupied
    w_t = w_ovov.reshape(cs, wb, occupied, pairs).transpose(2, 0, 3, 1)
    own_w = w_t.reshape(ZL * Y, rows, pairs * wb)
    swap_core = col_perm(lambda x, zh, c: (x, zh, c ^ 1))
    swap_x = col_perm(lambda x, zh, c: (x ^ 1, zh, c))
    swap_z = col_perm(lambda x, zh, c: (x, zh ^ 1, c))

    meets = [[row_perm(lambda z, q, f=f: (z, f(q))) for f in pair] for pair in MEETS]
    halves = [own[:1], own[1:]]
    got = [(own,)]
    near = {(0, 0): own_w}
    far = {}
    for step in range(1, Y // 2 + 1):
        moved = [lax.ppermute(h, "row", meets[n][(step + 1) % 2]) for n, h in enumerate(halves)]
        if step == 1:
            if GZ == 2:
                near[0, 1] = lax.ppermute(own_w, "col", swap_z)
            if GX == 2:
                near[1, 0] = lax.ppermute(own_w, "col", swap_x)
            *moved, held_w = lax.optimization_barrier((*moved, own_w))
            far[0, 0] = lax.ppermute(held_w, "col", swap_core)
            got[0] += tuple(moved)
            halves = [jnp.concatenate([h, m]) for h, m in zip(halves, moved)]
        else:
            got.append(tuple(moved))
            halves = moved
        if step == HOLD:
            keys = list(near)
            *halves, kept, w_last = lax.optimization_barrier((*halves, near[keys[-1]], near[keys[1]]))
            got[-1] = tuple(halves)
            near[keys[-1]], near[keys[1]] = kept, w_last
            if GX * GZ == 4:
                near[1, 1] = lax.ppermute(near[0, 1], "col", swap_x)
            for key in keys[1:]:
                far[key] = lax.ppermute(near[key], "col", swap_core)
    if GX * GZ == 4:
        far[1, 1] = lax.ppermute(near[1, 1], "col", swap_core)
    ws = [(far if dc else near)[dx, dz] for dx, dz, dc in FROM]

    acc = None
    for at, picks in PLAN:
        ts = [t for n in at for t in got[n]]
        acc = multiply(scalars, at, ts, ws, picks, acc, blocks)

    arrived = lax.all_to_all(acc, "col", 0, 0, tiled=True, axis_index_groups=PEER_GROUPS)
    total = jnp.sum(arrived, axis=0)
    run = virt // (X * ZH * CORES)
    return total.reshape(blocks, run, pairs, wb).transpose(1, 0, 2, 3)


def solution(mesh):
    return jax.shard_map(
        shards,
        mesh=mesh,
        in_specs=(P(None, "row", "col", None), P("col", "row", None)),
        out_specs=P("col", None, None, "row"),
        check_vma=False,
    )
```

```python
import functools

import jax
import jax.numpy as jnp
import numpy as np
from jax import lax
from jax.experimental import pallas as pl
from jax.experimental.pallas import tpu as pltpu
from jax.sharding import PartitionSpec as P

X, ZH, CORES = 8, 4, 2
ZL, Y = 2, 8
GX, GZ = 2, 1
XH, ZG = X // GX, ZH // GZ
MEMBERS = GX * GZ * CORES
PEERS = XH * ZG
F32 = jnp.float32
BF16 = jnp.bfloat16


def col_of(x, zh, core):
    return (x * ZH + zh) * CORES + core


def col_perm(move):
    pairs = []
    for x in range(X):
        for zh in range(ZH):
            for core in range(CORES):
                pairs.append((col_of(x, zh, core), col_of(*move(x, zh, core))))
    return pairs


def row_perm(move):
    pairs = []
    for zl in range(ZL):
        for y in range(Y):
            z2, y2 = move(zl, y)
            pairs.append((zl * Y + y, z2 * Y + y2 % Y))
    return pairs


GROUP = [(xl, zm, core) for xl in range(GX) for zm in range(GZ) for core in range(CORES)]
BASES = [(xh * GX, zg * GZ) for xh in range(XH) for zg in range(ZG)]
MEMBER_GROUPS = [
    [(zl * Y + y) * (X * ZH * CORES) + col_of(x + xl, zh + zm, core) for zl in range(ZL) for xl, zm, core in GROUP]
    for y in range(Y)
    for x, zh in BASES
]
PEER_GROUPS = [[col_of(x + xl, zh + zm, core) for x, zh in BASES] for xl, zm, core in GROUP]
NEAR = [(dx, dz) for dx in range(GX) for dz in range(GZ)]
FROM = [(dx, dz, dc) for dc in range(CORES) for dx, dz in NEAR]


def low_pair(y):
    return y ^ 1


def high_pair(y):
    return (y + 1 if y % 2 else y - 1) % Y


MEETS = [(low_pair, high_pair), (high_pair, low_pair)]


def sources(y):
    per_half = []
    for first, second in MEETS:
        steps = [[lambda q: q], [first]]
        held = steps[0] + steps[1]
        for n in range(2, Y // 2 + 1):
            meet = second if n % 2 == 0 else first
            held = [lambda q, f=f, meet=meet: f(meet(q)) for f in held]
            steps.append(held)
        per_half.append([[f(y) for f in step] for step in steps])
    zero, one = per_half
    calls = [[(0, y), (1, y)] + [(0, q) for q in zero[1]] + [(1, q) for q in one[1]]]
    for n in range(2, Y // 2 + 1):
        calls.append([(0, q) for q in zero[n]] + [(1, q) for q in one[n]])
    return calls


COUNTS = [len(call) for call in sources(0)]
SLOTS = sum(COUNTS)


PARTS = (2, 2)
EVERY = list(range(MEMBERS))


def row_table():
    table = np.zeros((ZL * Y, SLOTS), np.int32)
    for row in range(ZL * Y):
        table[row] = [zl * Y + q for call in sources(row % Y) for zl, q in call]
    return table


def col_table():
    table = np.zeros((X * ZH * CORES, MEMBERS), np.int32)
    for col in range(table.shape[0]):
        x, zh, core = col // (ZH * CORES) % GX, col // CORES % GZ, col % CORES
        table[col] = [((x ^ dx) * GZ + (zh ^ dz)) * CORES + (core ^ dc) for dx, dz, dc in FROM]
    return table


def split2(v):
    hi = v.astype(BF16)
    return hi, (v - hi.astype(F32)).astype(BF16)


def regroup_kernel(t_ref, out_ref):
    blocks, rows, virt = t_ref.shape
    run = virt // (X * ZH * CORES)
    src = lax.broadcasted_iota(jnp.int32, (virt, virt), 0)
    dst = lax.broadcasted_iota(jnp.int32, (virt, virt), 1)
    r = dst % run
    zg = (dst // run) % ZG
    xh = (dst // (run * ZG)) % XH
    core = (dst // (run * PEERS)) % CORES
    zm = (dst // (run * PEERS * CORES)) % GZ
    xl = dst // (run * PEERS * CORES * GZ)
    want = (((((xh * GX + xl) * ZG + zg) * GZ + zm) * CORES) + core) * run + r
    onehot = jnp.where(src == want, 1.0, 0.0).astype(BF16)
    width = virt // MEMBERS
    for i in range(blocks):
        v = t_ref[i]
        hi = v.astype(BF16)
        rest = v - hi.astype(F32)
        mid = rest.astype(BF16)
        low = (rest - mid.astype(F32)).astype(BF16)
        parts = jnp.dot(
            jnp.concatenate([hi, mid, low], axis=0), onehot, preferred_element_type=F32
        )
        moved = (parts[:rows] + parts[rows : 2 * rows]) + parts[2 * rows :]
        for m in range(MEMBERS):
            piece = moved[:, m * width : (m + 1) * width]
            for z in range(ZL):
                out_ref[z * MEMBERS + m, :, i * width : (i + 1) * width] = piece


def regroup(t):
    blocks, ks, cs, virt = t.shape
    rows = ks * cs
    return pl.pallas_call(
        regroup_kernel,
        out_shape=jax.ShapeDtypeStruct((ZL * MEMBERS, rows, blocks * virt // MEMBERS), F32),
        cost_estimate=pl.CostEstimate(flops=6 * blocks * rows * virt * virt, bytes_accessed=t.size * 8, transcendentals=0),
    )(t.reshape(blocks, rows, virt))


def multiply_kernel(has_acc, blocks, picks, n_t, n_w, *refs):
    s_ref = refs[0]
    t_refs = refs[1 : 1 + n_t]
    w_refs = refs[1 + n_t : 1 + n_t + n_w]
    out_ref = refs[-1]
    left = jnp.concatenate(
        [t[z, s_ref[SLOTS + n]] for t in t_refs for z in range(t.shape[0]) for n in picks], axis=0
    )
    right = jnp.concatenate([w[0] for w in w_refs], axis=0)
    lh, ll = split2(left)
    rh, rl = split2(right)
    total = lax.dot_general(
        jnp.concatenate([lh, lh, ll], axis=0),
        jnp.concatenate([rh, rl, rh], axis=0),
        (((0,), (0,)), ((), ())),
        preferred_element_type=F32,
    )
    run = total.shape[0] // (blocks * PEERS)
    total = total.reshape(blocks, PEERS, run, total.shape[1])
    for i in range(blocks):
        rows = slice(i * run, (i + 1) * run)
        if has_acc:
            out_ref[:, rows, :] = refs[1 + n_t + n_w][:, rows, :] + total[i]
        else:
            out_ref[:, rows, :] = total[i]


def multiply(scalars, at, ts, ws, picks, acc, blocks):
    ws = [ws[n] for n in picks]
    rows, width = ts[0].shape[2], ts[0].shape[3]
    wide = ws[0].shape[2]
    out_shape = (PEERS, width // PEERS, wide)
    slots = [sum(COUNTS[:n]) + m for n in at for m in range(COUNTS[n])]
    in_specs = [pl.BlockSpec(t.shape, lambda z, s: (0, 0, 0, 0)) for t in ts]
    in_specs += [
        pl.BlockSpec((1, rows, wide), lambda z, s, slot=slot: (s[slot], 0, 0)) for slot in slots for _ in ws
    ]
    args = [scalars, *ts, *(list(ws) * len(slots))]
    whole = pl.BlockSpec(out_shape, lambda z, s: (0, 0, 0))
    if acc is not None:
        in_specs.append(whole)
        args.append(acc)
    depth = len(slots) * len(ws) * rows
    return pl.pallas_call(
        functools.partial(multiply_kernel, acc is not None, blocks, picks, len(ts), len(slots) * len(ws)),
        grid_spec=pltpu.PrefetchScalarGridSpec(num_scalar_prefetch=1, grid=(1,), in_specs=in_specs, out_specs=whole),
        out_shape=jax.ShapeDtypeStruct(out_shape, F32),
        compiler_params=pltpu.CompilerParams(vmem_limit_bytes=32 * 2**20),
        cost_estimate=pl.CostEstimate(
            flops=6 * depth * width * wide, bytes_accessed=4 * depth * (width + wide), transcendentals=0
        ),
    )(*args)


def shards(t_pair, w_ovov):
    blocks, ks, cs, virt = t_pair.shape
    rows = ks * cs
    row, col = lax.axis_index("row"), lax.axis_index("col")
    scalars = jnp.concatenate(
        [
            lax.dynamic_index_in_dim(jnp.asarray(row_table()), row, keepdims=False),
            lax.dynamic_index_in_dim(jnp.asarray(col_table()), col, keepdims=False),
        ]
    )

    sent = regroup(t_pair)
    own = lax.all_to_all(
        sent, ("row", "col"), 0, 0, tiled=True, axis_index_groups=MEMBER_GROUPS
    ).reshape(ZL, MEMBERS, rows, -1)

    depth, wb, kj = w_ovov.shape
    occupied = ks * ZL * Y
    pairs = kj // occupied
    w_t = w_ovov.reshape(cs, wb, occupied, pairs).transpose(2, 0, 3, 1)
    own_w = w_t.reshape(ZL * Y, rows, pairs * wb)
    swap_core = col_perm(lambda x, zh, c: (x, zh, c ^ 1))
    swap_x = col_perm(lambda x, zh, c: (x ^ 1, zh, c))

    meets = [[row_perm(lambda z, q, f=f: (z, f(q))) for f in pair] for pair in MEETS]
    width = own.shape[3] // blocks
    near = {(0, 0): own_w}
    far = {}
    totals = []
    after = None
    first = 0
    for part, count in enumerate(PARTS):
        mine = own[:, :, :, first * width : (first + count) * width]
        first += count
        halves = [mine[:1], mine[1:]]
        if after is not None:
            *halves, _ = lax.optimization_barrier((*halves, after))
        got = [tuple(halves)]
        for step in range(1, Y // 2 + 1):
            moved = [lax.ppermute(h, "row", meets[n][(step + 1) % 2]) for n, h in enumerate(halves)]
            if part == 0 and step == 1:
                near[1, 0] = lax.ppermute(own_w, "col", swap_x)
                *moved, held_w = lax.optimization_barrier((*moved, own_w))
                far[0, 0] = lax.ppermute(held_w, "col", swap_core)
            if part == 0 and step == 2:
                *moved, near[1, 0] = lax.optimization_barrier((*moved, near[1, 0]))
                far[1, 0] = lax.ppermute(near[1, 0], "col", swap_core)
            if step == 3:
                *moved, after = lax.optimization_barrier((*moved, moved[0]))
            if step == 1:
                got[0] += tuple(moved)
                halves = [jnp.concatenate([h, m]) for h, m in zip(halves, moved)]
            else:
                got.append(tuple(moved))
                halves = moved
        ws = [(far if dc else near)[dx, dz] for dx, dz, dc in FROM]
        acc = None
        for at, ts in enumerate(got):
            acc = multiply(scalars, (at,), ts, ws, EVERY, acc, count)
        arrived = lax.all_to_all(acc, "col", 0, 0, tiled=True, axis_index_groups=PEER_GROUPS)
        totals.append(arrived)
    run = virt // (X * ZH * CORES)
    totals = [jnp.sum(t, axis=0).reshape(n, run, pairs, wb) for t, n in zip(totals, PARTS)]
    return jnp.concatenate(totals).transpose(1, 0, 2, 3)


def solution(mesh):
    return jax.shard_map(
        shards,
        mesh=mesh,
        in_specs=(P(None, "row", "col", None), P("col", "row", None)),
        out_specs=P("col", None, None, "row"),
        check_vma=False,
    )
```

```python
import functools

import jax
import jax.numpy as jnp
import numpy as np
from jax import lax
from jax.experimental import pallas as pl
from jax.experimental.pallas import tpu as pltpu
from jax.sharding import PartitionSpec as P

X, ZH, CORES = 8, 4, 2
ZL, Y = 2, 8
GX, GZ = 2, 2
XH, ZG = X // GX, ZH // GZ
MEMBERS = GX * GZ
PEERS = XH * ZG
F32 = jnp.float32
BF16 = jnp.bfloat16


def col_of(x, zh, core):
    return (x * ZH + zh) * CORES + core


def col_perm(move):
    pairs = []
    for x in range(X):
        for zh in range(ZH):
            for core in range(CORES):
                pairs.append((col_of(x, zh, core), col_of(*move(x, zh, core))))
    return pairs


def row_perm(move):
    pairs = []
    for zl in range(ZL):
        for y in range(Y):
            z2, y2 = move(zl, y)
            pairs.append((zl * Y + y, z2 * Y + y2 % Y))
    return pairs


GROUP = [(xl, zm) for xl in range(GX) for zm in range(GZ)]
BASES = [(xh * GX, zg * GZ) for xh in range(XH) for zg in range(ZG)]
MEMBER_GROUPS = [
    [(zl * Y + y) * (X * ZH * CORES) + col_of(x + xl, zh + zm, core) for zl in range(ZL) for xl, zm in GROUP]
    for y in range(Y)
    for x, zh in BASES
    for core in range(CORES)
]
PEER_GROUPS = [[col_of(x + xl, zh + zm, core) for x, zh in BASES] for xl, zm in GROUP for core in range(CORES)]
FROM = [(dx, dz) for dx in range(GX) for dz in range(GZ)]


def low_pair(y):
    return y ^ 1


def high_pair(y):
    return (y + 1 if y % 2 else y - 1) % Y


MEETS = [(low_pair, high_pair), (high_pair, low_pair)]


def sources(y):
    per_half = []
    for first, second in MEETS:
        steps = [[lambda q: q], [first]]
        held = steps[0] + steps[1]
        for n in range(2, Y // 2 + 1):
            meet = second if n % 2 == 0 else first
            held = [lambda q, f=f, meet=meet: f(meet(q)) for f in held]
            steps.append(held)
        per_half.append([[f(y) for f in step] for step in steps])
    zero, one = per_half
    calls = [[(0, y), (1, y)] + [(0, q) for q in zero[1]] + [(1, q) for q in one[1]]]
    for n in range(2, Y // 2 + 1):
        calls.append([(0, q) for q in zero[n]] + [(1, q) for q in one[n]])
    return calls


COUNTS = [len(call) for call in sources(0)]
SLOTS = sum(COUNTS)


EVERY = list(range(MEMBERS))
LATE = [n for n, (dx, dz) in enumerate(FROM) if dx + dz == 2]
EARLY = [n for n in EVERY if n not in LATE]
PLAN = [((0,), EARLY), ((1,), EARLY), ((2,), EARLY), ((0, 1, 2), LATE), ((3,), EVERY)]


def row_table():
    table = np.zeros((ZL * Y, SLOTS), np.int32)
    for row in range(ZL * Y):
        table[row] = [zl * Y + q for call in sources(row % Y) for zl, q in call]
    return table


def col_table():
    table = np.zeros((X * ZH * CORES, MEMBERS), np.int32)
    for col in range(table.shape[0]):
        x, zh = col // (ZH * CORES) % GX, col // CORES % GZ
        table[col] = [(x ^ dx) * GZ + (zh ^ dz) for dx, dz in FROM]
    return table


def split2(v):
    hi = v.astype(BF16)
    return hi, (v - hi.astype(F32)).astype(BF16)


def regroup_kernel(core_ref, t_ref, out_ref):
    blocks, rows, virt = t_ref.shape
    run = virt // (X * ZH * CORES)
    src = lax.broadcasted_iota(jnp.int32, (virt, virt), 0)
    dst = lax.broadcasted_iota(jnp.int32, (virt, virt), 1)
    r = dst % run
    zg = (dst // run) % ZG
    xh = (dst // (run * ZG)) % XH
    other = (dst // (run * PEERS)) % CORES
    core = (core_ref[0] + other) % CORES
    zm = (dst // (run * PEERS * CORES)) % GZ
    xl = dst // (run * PEERS * CORES * GZ)
    want = (((((xh * GX + xl) * ZG + zg) * GZ + zm) * CORES) + core) * run + r
    onehot = jnp.where(src == want, 1.0, 0.0).astype(BF16)
    width = virt // MEMBERS
    for i in range(blocks):
        v = t_ref[i]
        hi = v.astype(BF16)
        rest = v - hi.astype(F32)
        mid = rest.astype(BF16)
        low = (rest - mid.astype(F32)).astype(BF16)
        parts = jnp.dot(
            jnp.concatenate([hi, mid, low], axis=0), onehot, preferred_element_type=F32
        )
        moved = (parts[:rows] + parts[rows : 2 * rows]) + parts[2 * rows :]
        for m in range(MEMBERS):
            piece = moved[:, m * width : (m + 1) * width]
            for z in range(ZL):
                out_ref[z * MEMBERS + m, :, i * width : (i + 1) * width] = piece


def regroup(t, core):
    blocks, ks, cs, virt = t.shape
    rows = ks * cs
    return pl.pallas_call(
        regroup_kernel,
        in_specs=[pl.BlockSpec(memory_space=pltpu.SMEM), pl.BlockSpec(memory_space=pltpu.VMEM)],
        out_shape=jax.ShapeDtypeStruct((ZL * MEMBERS, rows, blocks * virt // MEMBERS), F32),
        cost_estimate=pl.CostEstimate(flops=6 * blocks * rows * virt * virt, bytes_accessed=t.size * 8, transcendentals=0),
    )(core.reshape(1), t.reshape(blocks, rows, virt))


def multiply_kernel(has_acc, blocks, picks, n_t, n_w, *refs):
    s_ref = refs[0]
    t_refs = refs[1 : 1 + n_t]
    w_refs = refs[1 + n_t : 1 + n_t + n_w]
    accs = refs[1 + n_t + n_w : -CORES]
    outs = refs[-CORES:]
    left = jnp.concatenate(
        [t[z, s_ref[SLOTS + n]] for t in t_refs for z in range(t.shape[0]) for n in picks], axis=0
    )
    right = jnp.concatenate([w[0] for w in w_refs], axis=0)
    lh, ll = split2(left)
    rh, rl = split2(right)
    total = lax.dot_general(
        jnp.concatenate([lh, lh, ll], axis=0),
        jnp.concatenate([rh, rl, rh], axis=0),
        (((0,), (0,)), ((), ())),
        preferred_element_type=F32,
    )
    run = total.shape[0] // (blocks * CORES * PEERS)
    total = total.reshape(blocks, CORES, PEERS, run, total.shape[1])
    for i in range(blocks):
        rows = slice(i * run, (i + 1) * run)
        for c in range(CORES):
            if has_acc:
                outs[c][:, rows, :] = accs[c][:, rows, :] + total[i, c]
            else:
                outs[c][:, rows, :] = total[i, c]


def multiply(scalars, at, ts, ws, picks, acc, blocks):
    ws = [ws[n] for n in picks]
    rows, width = ts[0].shape[2], ts[0].shape[3]
    wide = ws[0].shape[2]
    out_shape = (PEERS, width // (CORES * PEERS), wide)
    slots = [sum(COUNTS[:n]) + m for n in at for m in range(COUNTS[n])]
    in_specs = [pl.BlockSpec(t.shape, lambda z, s: (0, 0, 0, 0)) for t in ts]
    in_specs += [
        pl.BlockSpec((1, rows, wide), lambda z, s, slot=slot: (s[slot], 0, 0)) for slot in slots for _ in ws
    ]
    args = [scalars, *ts, *(list(ws) * len(slots))]
    whole = pl.BlockSpec(out_shape, lambda z, s: (0, 0, 0))
    if acc is not None:
        in_specs += [whole] * CORES
        args += acc
    depth = len(slots) * len(ws) * rows
    return pl.pallas_call(
        functools.partial(multiply_kernel, acc is not None, blocks, picks, len(ts), len(slots) * len(ws)),
        grid_spec=pltpu.PrefetchScalarGridSpec(num_scalar_prefetch=1, grid=(1,), in_specs=in_specs, out_specs=[whole] * CORES),
        out_shape=[jax.ShapeDtypeStruct(out_shape, F32)] * CORES,
        compiler_params=pltpu.CompilerParams(vmem_limit_bytes=32 * 2**20),
        cost_estimate=pl.CostEstimate(
            flops=6 * depth * width * wide, bytes_accessed=4 * depth * (width + wide), transcendentals=0
        ),
    )(*args)


def shards(t_pair, w_ovov):
    blocks, ks, cs, virt = t_pair.shape
    rows = ks * cs
    row, col = lax.axis_index("row"), lax.axis_index("col")
    scalars = jnp.concatenate(
        [
            lax.dynamic_index_in_dim(jnp.asarray(row_table()), row, keepdims=False),
            lax.dynamic_index_in_dim(jnp.asarray(col_table()), col, keepdims=False),
        ]
    )

    sent = regroup(t_pair, (col % CORES).astype(jnp.int32))
    own = lax.all_to_all(
        sent, ("row", "col"), 0, 0, tiled=True, axis_index_groups=MEMBER_GROUPS
    ).reshape(ZL, MEMBERS, rows, -1)

    depth, wb, kj = w_ovov.shape
    occupied = ks * ZL * Y
    pairs = kj // occupied
    w_t = w_ovov.reshape(cs, wb, occupied, pairs).transpose(2, 0, 3, 1)
    own_w = w_t.reshape(ZL * Y, rows, pairs * wb)
    first_w = own_w
    own, own_w = lax.optimization_barrier((own, own_w))
    swap_core = col_perm(lambda x, zh, c: (x, zh, c ^ 1))
    swap_x = col_perm(lambda x, zh, c: (x ^ 1, zh, c))
    swap_z = col_perm(lambda x, zh, c: (x, zh ^ 1, c))

    meets = [[row_perm(lambda z, q, f=f: (z, f(q))) for f in pair] for pair in MEETS]
    halves = [own[:1], own[1:]]
    got = [(own,)]
    near = {(0, 0): own_w, (0, 1): lax.ppermute(first_w, "col", swap_z)}
    for step in range(1, Y // 2 + 1):
        moved = [lax.ppermute(h, "row", meets[n][(step + 1) % 2]) for n, h in enumerate(halves)]
        if step == 1:
            *moved, held = lax.optimization_barrier((*moved, own_w))
            near[1, 0] = lax.ppermute(held, "col", swap_x)
        if step == 3:
            *moved, near[0, 1] = lax.optimization_barrier((*moved, near[0, 1]))
            near[1, 1] = lax.ppermute(near[0, 1], "col", swap_x)
        if step == 1:
            got[0] += tuple(moved)
            halves = [jnp.concatenate([h, m]) for h, m in zip(halves, moved)]
        else:
            got.append(tuple(moved))
            halves = moved
    ws = [near[key] for key in FROM]

    acc = None
    for at, picks in PLAN:
        ts = [t for n in at for t in got[n]]
        acc = multiply(scalars, at, ts, ws, picks, acc, blocks)

    acc = acc[0] + lax.ppermute(acc[1], "col", swap_core)
    arrived = lax.all_to_all(acc, "col", 0, 0, tiled=True, axis_index_groups=PEER_GROUPS)
    total = jnp.sum(arrived, axis=0)
    run = virt // (X * ZH * CORES)
    return total.reshape(blocks, run, pairs, wb).transpose(1, 0, 2, 3)


def solution(mesh):
    return jax.shard_map(
        shards,
        mesh=mesh,
        in_specs=(P(None, "row", "col", None), P("col", "row", None)),
        out_specs=P("col", None, None, "row"),
        check_vma=False,
    )
```

```python
import functools

import jax
import jax.numpy as jnp
import numpy as np
from jax import lax
from jax.experimental import pallas as pl
from jax.experimental.pallas import tpu as pltpu
from jax.sharding import PartitionSpec as P

X, ZH, CORES = 8, 4, 2
ZL, Y = 2, 8
GX = 2
XH = X // GX
MEMBERS = GX * CORES
PEERS = XH * ZH
F32 = jnp.float32
BF16 = jnp.bfloat16


def col_of(x, zh, core):
    return (x * ZH + zh) * CORES + core


def col_perm(move):
    pairs = []
    for x in range(X):
        for zh in range(ZH):
            for core in range(CORES):
                pairs.append((col_of(x, zh, core), col_of(*move(x, zh, core))))
    return pairs


def row_perm(move):
    pairs = []
    for zl in range(ZL):
        for y in range(Y):
            z2, y2 = move(zl, y)
            pairs.append((zl * Y + y, z2 * Y + y2 % Y))
    return pairs


MEMBER_GROUPS = [
    [
        (zl * Y + y) * (X * ZH * CORES) + col_of(xh * GX + xl, zh, core)
        for zl in range(ZL)
        for xl in range(GX)
        for core in range(CORES)
    ]
    for y in range(Y)
    for xh in range(XH)
    for zh in range(ZH)
]
PEER_GROUPS = [
    [col_of(xh * GX + xl, zh, core) for xh in range(XH) for zh in range(ZH)]
    for xl in range(GX)
    for core in range(CORES)
]


def low_pair(y):
    return y ^ 1


def high_pair(y):
    return (y + 1 if y % 2 else y - 1) % Y


MEETS = [(low_pair, high_pair), (high_pair, low_pair)]


def sources(y):
    per_half = []
    for first, second in MEETS:
        steps = [[lambda q: q], [first]]
        held = steps[0] + steps[1]
        for n in range(2, Y // 2 + 1):
            meet = second if n % 2 == 0 else first
            held = [lambda q, f=f, meet=meet: f(meet(q)) for f in held]
            steps.append(held)
        per_half.append([[f(y) for f in step] for step in steps])
    zero, one = per_half
    calls = [[(0, y), (1, y)] + [(0, q) for q in zero[1]] + [(1, q) for q in one[1]]]
    for n in range(2, Y // 2 + 1):
        calls.append([(0, q) for q in zero[n]] + [(1, q) for q in one[n]])
    return calls


COUNTS = [len(call) for call in sources(0)]
SLOTS = sum(COUNTS)


def row_table():
    table = np.zeros((ZL * Y, SLOTS), np.int32)
    for row in range(ZL * Y):
        table[row] = [zl * Y + q for call in sources(row % Y) for zl, q in call]
    return table


def col_table():
    table = np.zeros((X * ZH * CORES, MEMBERS), np.int32)
    for col in range(table.shape[0]):
        x, core = col // (ZH * CORES), col % CORES
        for n in range(MEMBERS):
            source = (x - n % GX) % GX
            table[col, n] = source * CORES + (core if n < GX else 1 - core)
    return table


def split2(v):
    hi = v.astype(BF16)
    return hi, (v - hi.astype(F32)).astype(BF16)


def regroup_kernel(t_ref, out_ref):
    blocks, rows, virt = t_ref.shape[0], t_ref.shape[1], t_ref.shape[2]
    run = virt // (X * ZH * CORES)
    src = lax.broadcasted_iota(jnp.int32, (virt, virt), 0)
    dst = lax.broadcasted_iota(jnp.int32, (virt, virt), 1)
    r = dst % run
    zh = (dst // run) % ZH
    xh = (dst // (run * ZH)) % XH
    core = (dst // (run * ZH * XH)) % CORES
    xl = dst // (run * ZH * XH * CORES)
    want = ((((xh * GX + xl) * ZH + zh) * CORES) + core) * run + r
    onehot = jnp.where(src == want, 1.0, 0.0).astype(BF16)
    width = virt // MEMBERS
    for i in range(blocks):
        v = t_ref[i]
        hi = v.astype(BF16)
        rest = v - hi.astype(F32)
        mid = rest.astype(BF16)
        low = (rest - mid.astype(F32)).astype(BF16)
        parts = jnp.dot(
            jnp.concatenate([hi, mid, low], axis=0), onehot, preferred_element_type=F32
        )
        moved = (parts[:rows] + parts[rows : 2 * rows]) + parts[2 * rows :]
        for m in range(MEMBERS):
            piece = moved[:, m * width : (m + 1) * width]
            for z in range(ZL):
                out_ref[z * MEMBERS + m, :, i * width : (i + 1) * width] = piece


def regroup(t):
    blocks, ks, cs, virt = t.shape
    rows = ks * cs
    return pl.pallas_call(
        regroup_kernel,
        out_shape=jax.ShapeDtypeStruct((ZL * MEMBERS, rows, blocks * virt // MEMBERS), F32),
        cost_estimate=pl.CostEstimate(flops=6 * blocks * rows * virt * virt, bytes_accessed=t.size * 8, transcendentals=0),
    )(t.reshape(blocks, rows, virt))


def multiply_kernel(has_acc, blocks, order_at, n_t, n_w, *refs):
    s_ref = refs[0]
    t_refs = refs[1 : 1 + n_t]
    w_refs = refs[1 + n_t : 1 + n_t + n_w]
    out_ref = refs[-1]
    left = jnp.concatenate(
        [t[z, s_ref[order_at + n]] for t in t_refs for z in range(t.shape[0]) for n in range(MEMBERS)], axis=0
    )
    right = jnp.concatenate([w[0] for w in w_refs], axis=0)
    lh, ll = split2(left)
    rh, rl = split2(right)
    total = lax.dot_general(
        jnp.concatenate([lh, lh, ll], axis=0),
        jnp.concatenate([rh, rl, rh], axis=0),
        (((0,), (0,)), ((), ())),
        preferred_element_type=F32,
    )
    run = total.shape[0] // (blocks * PEERS)
    total = total.reshape(blocks, PEERS, run, total.shape[1])
    for i in range(blocks):
        rows = slice(i * run, (i + 1) * run)
        if has_acc:
            out_ref[:, rows, :] = refs[1 + n_t + n_w][:, rows, :] + total[i]
        else:
            out_ref[:, rows, :] = total[i]


def multiply(scalars, at, ts, ws, acc, blocks):
    rows, width = ts[0].shape[2], ts[0].shape[3]
    wide = ws[0].shape[2]
    out_shape = (PEERS, width // PEERS, wide)
    first = sum(COUNTS[:at])
    slots = range(first, first + COUNTS[at])
    in_specs = [pl.BlockSpec(t.shape, lambda z, s: (0, 0, 0, 0)) for t in ts]
    in_specs += [
        pl.BlockSpec((1, rows, wide), lambda z, s, slot=slot: (s[slot], 0, 0)) for slot in slots for _ in ws
    ]
    args = [scalars, *ts, *(list(ws) * len(slots))]
    whole = pl.BlockSpec(out_shape, lambda z, s: (0, 0, 0))
    if acc is not None:
        in_specs.append(whole)
        args.append(acc)
    depth = len(slots) * len(ws) * rows
    return pl.pallas_call(
        functools.partial(multiply_kernel, acc is not None, blocks, SLOTS, len(ts), len(slots) * len(ws)),
        grid_spec=pltpu.PrefetchScalarGridSpec(num_scalar_prefetch=1, grid=(1,), in_specs=in_specs, out_specs=whole),
        out_shape=jax.ShapeDtypeStruct(out_shape, F32),
        compiler_params=pltpu.CompilerParams(vmem_limit_bytes=32 * 2**20),
        cost_estimate=pl.CostEstimate(
            flops=6 * depth * width * wide, bytes_accessed=4 * depth * (width + wide), transcendentals=0
        ),
    )(*args)


def shards(t_pair, w_ovov):
    blocks, ks, cs, virt = t_pair.shape
    rows = ks * cs
    row, col = lax.axis_index("row"), lax.axis_index("col")
    scalars = jnp.concatenate(
        [
            lax.dynamic_index_in_dim(jnp.asarray(row_table()), row, keepdims=False),
            lax.dynamic_index_in_dim(jnp.asarray(col_table()), col, keepdims=False),
        ]
    )

    sent = regroup(t_pair)
    own = lax.all_to_all(
        sent, ("row", "col"), 0, 0, tiled=True, axis_index_groups=MEMBER_GROUPS
    ).reshape(ZL, MEMBERS, rows, -1)

    depth, wb, kj = w_ovov.shape
    occupied = ks * ZL * Y
    pairs = kj // occupied
    own_w = w_ovov.reshape(cs, wb, occupied, pairs).transpose(2, 0, 3, 1).reshape(ZL * Y, rows, pairs * wb)
    own, own_w = lax.optimization_barrier((own, own_w))
    swap_core = col_perm(lambda x, zh, c: (x, zh, 1 - c))
    swap_x = col_perm(lambda x, zh, c: (x ^ 1, zh, c))
    w_x = lax.ppermute(own_w, "col", swap_x)

    meets = [[row_perm(lambda z, q, f=f: (z, f(q))) for f in pair] for pair in MEETS]
    halves = [own[:1], own[1:]]
    got = [(own,)]
    for step in range(1, Y // 2 + 1):
        moved = [lax.ppermute(h, "row", meets[n][(step + 1) % 2]) for n, h in enumerate(halves)]
        if step == 1:
            *moved, held_w = lax.optimization_barrier((*moved, own_w))
            w_c = lax.ppermute(held_w, "col", swap_core)
            got[0] += tuple(moved)
            halves = [jnp.concatenate([h, m]) for h, m in zip(halves, moved)]
        else:
            got.append(tuple(moved))
            halves = moved
        if step == 2:
            *halves, w_x, w_c = lax.optimization_barrier((*halves, w_x, w_c))
            got[-1] = tuple(halves)
    w_xc = lax.ppermute(w_x, "col", swap_core)
    ws = [own_w, w_x, w_c, w_xc]

    acc = None
    for at, ts in enumerate(got):
        acc = multiply(scalars, at, ts, ws, acc, blocks)

    arrived = lax.all_to_all(acc, "col", 0, 0, tiled=True, axis_index_groups=PEER_GROUPS)
    total = jnp.sum(arrived, axis=0)
    run = virt // (X * ZH * CORES)
    return total.reshape(blocks, run, pairs, wb).transpose(1, 0, 2, 3)


def solution(mesh):
    return jax.shard_map(
        shards,
        mesh=mesh,
        in_specs=(P(None, "row", "col", None), P("col", "row", None)),
        out_specs=P("col", None, None, "row"),
        check_vma=False,
    )
```

```python
import functools

import jax
import jax.numpy as jnp
import numpy as np
from jax import lax
from jax.experimental import pallas as pl
from jax.experimental.pallas import tpu as pltpu
from jax.sharding import PartitionSpec as P

X, ZH, CORES = 8, 4, 2
ZL, Y = 2, 8
GX = 2
XH = X // GX
MEMBERS = GX * CORES
PEERS = XH * ZH
LANES = 128
F32 = jnp.float32
BF16 = jnp.bfloat16


def col_of(x, zh, core):
    return (x * ZH + zh) * CORES + core


def col_perm(move):
    pairs = []
    for x in range(X):
        for zh in range(ZH):
            for core in range(CORES):
                pairs.append((col_of(x, zh, core), col_of(*move(x, zh, core))))
    return pairs


def row_perm(move):
    pairs = []
    for zl in range(ZL):
        for y in range(Y):
            z2, y2 = move(zl, y)
            pairs.append((zl * Y + y, z2 * Y + y2 % Y))
    return pairs


MEMBER_GROUPS = [
    [
        (zl * Y + y) * (X * ZH * CORES) + col_of(xh * GX + xl, zh, core)
        for zl in range(ZL)
        for xl in range(GX)
        for core in range(CORES)
    ]
    for y in range(Y)
    for xh in range(XH)
    for zh in range(ZH)
]
PEER_GROUPS = [
    [col_of(xh * GX + xl, zh, core) for xh in range(XH) for zh in range(ZH)]
    for xl in range(GX)
    for core in range(CORES)
]


def low_pair(y):
    return y ^ 1


def high_pair(y):
    return (y + 1 if y % 2 else y - 1) % Y


MEETS = [(low_pair, high_pair), (high_pair, low_pair)]


def sources(y):
    per_half = []
    for first, second in MEETS:
        steps = [[lambda q: q], [first]]
        held = steps[0] + steps[1]
        for n in range(2, Y // 2 + 1):
            meet = second if n % 2 == 0 else first
            held = [lambda q, f=f, meet=meet: f(meet(q)) for f in held]
            steps.append(held)
        per_half.append([[f(y) for f in step] for step in steps])
    zero, one = per_half
    calls = [[(0, y), (1, y)] + [(0, q) for q in zero[1]] + [(1, q) for q in one[1]]]
    for n in range(2, Y // 2 + 1):
        calls.append([(0, q) for q in zero[n]] + [(1, q) for q in one[n]])
    return calls


COUNTS = [len(call) for call in sources(0)]
SLOTS = sum(COUNTS)


def row_table():
    table = np.zeros((ZL * Y, SLOTS), np.int32)
    for row in range(ZL * Y):
        table[row] = [zl * Y + q for call in sources(row % Y) for zl, q in call]
    return table


def col_table():
    table = np.zeros((X * ZH * CORES, MEMBERS), np.int32)
    for col in range(table.shape[0]):
        x, core = col // (ZH * CORES), col % CORES
        for n in range(MEMBERS):
            source = (x - n % GX) % GX
            table[col, n] = source * CORES + (core if n < GX else 1 - core)
    return table


def split2(v):
    hi = v.astype(BF16)
    return hi, (v - hi.astype(F32)).astype(BF16)


def regroup_kernel(t_ref, out_ref):
    blocks, rows, virt = t_ref.shape[0], t_ref.shape[1], t_ref.shape[2]
    run = virt // (X * ZH * CORES)
    src = lax.broadcasted_iota(jnp.int32, (virt, virt), 0)
    dst = lax.broadcasted_iota(jnp.int32, (virt, virt), 1)
    r = dst % run
    zh = (dst // run) % ZH
    xh = (dst // (run * ZH)) % XH
    core = (dst // (run * ZH * XH)) % CORES
    xl = dst // (run * ZH * XH * CORES)
    want = ((((xh * GX + xl) * ZH + zh) * CORES) + core) * run + r
    onehot = jnp.where(src == want, 1.0, 0.0).astype(BF16)
    width = virt // MEMBERS
    for i in range(blocks):
        v = t_ref[i]
        hi = v.astype(BF16)
        rest = v - hi.astype(F32)
        mid = rest.astype(BF16)
        low = (rest - mid.astype(F32)).astype(BF16)
        parts = jnp.dot(
            jnp.concatenate([hi, mid, low], axis=0), onehot, preferred_element_type=F32
        )
        moved = (parts[:rows] + parts[rows : 2 * rows]) + parts[2 * rows :]
        for m in range(MEMBERS):
            piece = moved[:, m * width : (m + 1) * width]
            for z in range(ZL):
                out_ref[z * MEMBERS + m, :, i * width : (i + 1) * width] = piece


def regroup(t):
    blocks, ks, cs, virt = t.shape
    rows = ks * cs
    return pl.pallas_call(
        regroup_kernel,
        out_shape=jax.ShapeDtypeStruct((ZL * MEMBERS, rows, blocks * virt // MEMBERS), F32),
        cost_estimate=pl.CostEstimate(flops=6 * blocks * rows * virt * virt, bytes_accessed=t.size * 8, transcendentals=0),
    )(t.reshape(blocks, rows, virt))


def arrange_kernel(pairs, wb, w_ref, out_ref, mid_ref, onehot_ref):
    ks = LANES // pairs
    cs = w_ref.shape[0] // wb
    wide = pairs * wb

    @pl.when(pl.program_id(0) == 0)
    def _():
        src = lax.broadcasted_iota(jnp.int32, (wide, wide), 0)
        dst = lax.broadcasted_iota(jnp.int32, (wide, wide), 1)
        onehot_ref[...] = jnp.where(src == dst % wb * pairs + dst // wb, 1.0, 0.0).astype(BF16)

    run = lax.broadcasted_iota(jnp.int32, (cs, LANES), 1) // pairs
    for h in range(wb // ks):
        tiles = [w_ref[pl.ds(h * ks + n, cs, stride=wb), :] for n in range(ks)]
        d = 1
        while d < ks:
            low = run // d % 2 == 0
            for n in range(ks):
                if n // d % 2 == 0:
                    a, b = tiles[n], tiles[n + d]
                    tiles[n] = jnp.where(low, a, pltpu.roll(b, d * pairs, 1))
                    tiles[n + d] = jnp.where(low, pltpu.roll(a, LANES - d * pairs, 1), b)
            d *= 2
        for n in range(ks):
            mid_ref[n * cs : (n + 1) * cs, h * LANES : (h + 1) * LANES] = tiles[n]
    v = mid_ref[...]
    hi = v.astype(BF16)
    rest = v - hi.astype(F32)
    mid = rest.astype(BF16)
    low = (rest - mid.astype(F32)).astype(BF16)
    n = v.shape[0]
    got = jnp.dot(jnp.concatenate([hi, mid, low], axis=0), onehot_ref[...], preferred_element_type=F32)
    out_ref[...] = ((got[:n] + got[n : 2 * n]) + got[2 * n :]).reshape(out_ref.shape)


def arrange(w, occupied, rows_of):
    cs, wb, kj = w.shape
    pairs = kj // occupied
    blocks = occupied * cs // rows_of
    steps = kj // LANES
    return pl.pallas_call(
        functools.partial(arrange_kernel, pairs, wb),
        grid=(steps,),
        in_specs=[pl.BlockSpec((cs * wb, LANES), lambda g: (0, g))],
        out_specs=pl.BlockSpec((blocks // steps, rows_of, pairs * wb), lambda g: (g, 0, 0)),
        out_shape=jax.ShapeDtypeStruct((blocks, rows_of, pairs * wb), F32),
        scratch_shapes=[
            pltpu.VMEM((LANES // pairs * cs, pairs * wb), F32),
            pltpu.VMEM((pairs * wb, pairs * wb), BF16),
        ],
        cost_estimate=pl.CostEstimate(
            flops=6 * occupied * cs * (pairs * wb) ** 2, bytes_accessed=8 * w.size, transcendentals=0
        ),
    )(w.reshape(cs * wb, kj))


def multiply_kernel(has_acc, blocks, order_at, n_t, n_w, *refs):
    s_ref = refs[0]
    t_refs = refs[1 : 1 + n_t]
    w_refs = refs[1 + n_t : 1 + n_t + n_w]
    out_ref = refs[-1]
    left = jnp.concatenate(
        [t[z, s_ref[order_at + n]] for t in t_refs for z in range(t.shape[0]) for n in range(MEMBERS)], axis=0
    )
    right = jnp.concatenate([w[0] for w in w_refs], axis=0)
    lh, ll = split2(left)
    rh, rl = split2(right)
    total = lax.dot_general(
        jnp.concatenate([lh, lh, ll], axis=0),
        jnp.concatenate([rh, rl, rh], axis=0),
        (((0,), (0,)), ((), ())),
        preferred_element_type=F32,
    )
    run = total.shape[0] // (blocks * PEERS)
    total = total.reshape(blocks, PEERS, run, total.shape[1])
    for i in range(blocks):
        rows = slice(i * run, (i + 1) * run)
        if has_acc:
            out_ref[:, rows, :] = refs[1 + n_t + n_w][:, rows, :] + total[i]
        else:
            out_ref[:, rows, :] = total[i]


def multiply(scalars, at, ts, ws, acc, blocks):
    rows, width = ts[0].shape[2], ts[0].shape[3]
    wide = ws[0].shape[2]
    out_shape = (PEERS, width // PEERS, wide)
    first = sum(COUNTS[:at])
    slots = range(first, first + COUNTS[at])
    in_specs = [pl.BlockSpec(t.shape, lambda z, s: (0, 0, 0, 0)) for t in ts]
    in_specs += [
        pl.BlockSpec((1, rows, wide), lambda z, s, slot=slot: (s[slot], 0, 0)) for slot in slots for _ in ws
    ]
    args = [scalars, *ts, *(list(ws) * len(slots))]
    whole = pl.BlockSpec(out_shape, lambda z, s: (0, 0, 0))
    if acc is not None:
        in_specs.append(whole)
        args.append(acc)
    depth = len(slots) * len(ws) * rows
    return pl.pallas_call(
        functools.partial(multiply_kernel, acc is not None, blocks, SLOTS, len(ts), len(slots) * len(ws)),
        grid_spec=pltpu.PrefetchScalarGridSpec(num_scalar_prefetch=1, grid=(1,), in_specs=in_specs, out_specs=whole),
        out_shape=jax.ShapeDtypeStruct(out_shape, F32),
        compiler_params=pltpu.CompilerParams(vmem_limit_bytes=32 * 2**20),
        cost_estimate=pl.CostEstimate(
            flops=6 * depth * width * wide, bytes_accessed=4 * depth * (width + wide), transcendentals=0
        ),
    )(*args)


def shards(t_pair, w_ovov):
    blocks, ks, cs, virt = t_pair.shape
    rows = ks * cs
    row, col = lax.axis_index("row"), lax.axis_index("col")
    scalars = jnp.concatenate(
        [
            lax.dynamic_index_in_dim(jnp.asarray(row_table()), row, keepdims=False),
            lax.dynamic_index_in_dim(jnp.asarray(col_table()), col, keepdims=False),
        ]
    )

    sent = regroup(t_pair)
    own = lax.all_to_all(
        sent, ("row", "col"), 0, 0, tiled=True, axis_index_groups=MEMBER_GROUPS
    ).reshape(ZL, MEMBERS, rows, -1)

    depth, wb, kj = w_ovov.shape
    occupied = ks * ZL * Y
    pairs = kj // occupied
    own_w = arrange(w_ovov, occupied, rows)
    swap_core = col_perm(lambda x, zh, c: (x, zh, 1 - c))
    swap_x = col_perm(lambda x, zh, c: (x ^ 1, zh, c))
    w_x = lax.ppermute(own_w, "col", swap_x)
    w_c = lax.ppermute(own_w, "col", swap_core)

    meets = [[row_perm(lambda z, q, f=f: (z, f(q))) for f in pair] for pair in MEETS]
    halves = [own[:1], own[1:]]
    got = [(own,)]
    for step in range(1, Y // 2 + 1):
        moved = [lax.ppermute(h, "row", meets[n][(step + 1) % 2]) for n, h in enumerate(halves)]
        if step == 1:
            got[0] += tuple(moved)
            halves = [jnp.concatenate([h, m]) for h, m in zip(halves, moved)]
        else:
            got.append(tuple(moved))
            halves = moved
        if step == 2:
            *halves, w_x, w_c = lax.optimization_barrier((*halves, w_x, w_c))
            got[-1] = tuple(halves)
    w_xc = lax.ppermute(w_x, "col", swap_core)
    ws = [own_w, w_x, w_c, w_xc]

    acc = None
    for at, ts in enumerate(got):
        acc = multiply(scalars, at, ts, ws, acc, blocks)

    arrived = lax.all_to_all(acc, "col", 0, 0, tiled=True, axis_index_groups=PEER_GROUPS)
    total = jnp.sum(arrived, axis=0)
    run = virt // (X * ZH * CORES)
    return total.reshape(blocks, run, pairs, wb).transpose(1, 0, 2, 3)


def solution(mesh):
    return jax.shard_map(
        shards,
        mesh=mesh,
        in_specs=(P(None, "row", "col", None), P("col", "row", None)),
        out_specs=P("col", None, None, "row"),
        check_vma=False,
    )
```

```python
import functools

import jax
import jax.numpy as jnp
import numpy as np
from jax import lax
from jax.experimental import pallas as pl
from jax.experimental.pallas import tpu as pltpu
from jax.sharding import PartitionSpec as P

X, ZH, CORES = 8, 4, 2
ZL, Y = 2, 8
GX, GZ = 2, 2
XH, ZG = X // GX, ZH // GZ
MEMBERS = GX * GZ
PEERS = XH * ZG
LANES = 128
F32 = jnp.float32
BF16 = jnp.bfloat16


def col_of(x, zh, core):
    return (x * ZH + zh) * CORES + core


def col_perm(move):
    pairs = []
    for x in range(X):
        for zh in range(ZH):
            for core in range(CORES):
                pairs.append((col_of(x, zh, core), col_of(*move(x, zh, core))))
    return pairs


def row_perm(move):
    pairs = []
    for zl in range(ZL):
        for y in range(Y):
            z2, y2 = move(zl, y)
            pairs.append((zl * Y + y, z2 * Y + y2 % Y))
    return pairs


GROUP = [(xl, zm) for xl in range(GX) for zm in range(GZ)]
BASES = [(xh * GX, zg * GZ) for xh in range(XH) for zg in range(ZG)]
MEMBER_GROUPS = [
    [(zl * Y + y) * (X * ZH * CORES) + col_of(x + xl, zh + zm, core) for zl in range(ZL) for xl, zm in GROUP]
    for y in range(Y)
    for x, zh in BASES
    for core in range(CORES)
]
PEER_GROUPS = [[col_of(x + xl, zh + zm, core) for x, zh in BASES] for xl, zm in GROUP for core in range(CORES)]
FROM = [(dx, dz) for dx in range(GX) for dz in range(GZ)]


def low_pair(y):
    return y ^ 1


def high_pair(y):
    return (y + 1 if y % 2 else y - 1) % Y


MEETS = [(low_pair, high_pair), (high_pair, low_pair)]


def sources(y):
    per_half = []
    for first, second in MEETS:
        steps = [[lambda q: q], [first]]
        held = steps[0] + steps[1]
        for n in range(2, Y // 2 + 1):
            meet = second if n % 2 == 0 else first
            held = [lambda q, f=f, meet=meet: f(meet(q)) for f in held]
            steps.append(held)
        per_half.append([[f(y) for f in step] for step in steps])
    zero, one = per_half
    calls = [[(0, y), (1, y)] + [(0, q) for q in zero[1]] + [(1, q) for q in one[1]]]
    for n in range(2, Y // 2 + 1):
        calls.append([(0, q) for q in zero[n]] + [(1, q) for q in one[n]])
    return calls


COUNTS = [len(call) for call in sources(0)]
SLOTS = sum(COUNTS)


HOLD = 2
EVERY = list(range(MEMBERS))
LATE = [n for n, (dx, dz) in enumerate(FROM) if dx + dz == 2]
EARLY = [n for n in EVERY if n not in LATE]
PLAN = [((0,), EARLY), ((1,), EARLY), ((2,), EARLY), ((3,), EARLY), ((0, 1, 2, 3), LATE)]


def row_table():
    table = np.zeros((ZL * Y, SLOTS), np.int32)
    for row in range(ZL * Y):
        table[row] = [zl * Y + q for call in sources(row % Y) for zl, q in call]
    return table


def col_table():
    table = np.zeros((X * ZH * CORES, MEMBERS), np.int32)
    for col in range(table.shape[0]):
        x, zh = col // (ZH * CORES) % GX, col // CORES % GZ
        table[col] = [(x ^ dx) * GZ + (zh ^ dz) for dx, dz in FROM]
    return table


def split2(v):
    hi = v.astype(BF16)
    return hi, (v - hi.astype(F32)).astype(BF16)


def regroup_kernel(core_ref, t_ref, out_ref):
    blocks, rows, virt = t_ref.shape
    run = virt // (X * ZH * CORES)
    src = lax.broadcasted_iota(jnp.int32, (virt, virt), 0)
    dst = lax.broadcasted_iota(jnp.int32, (virt, virt), 1)
    r = dst % run
    zg = (dst // run) % ZG
    xh = (dst // (run * ZG)) % XH
    other = (dst // (run * PEERS)) % CORES
    core = (core_ref[0] + other) % CORES
    zm = (dst // (run * PEERS * CORES)) % GZ
    xl = dst // (run * PEERS * CORES * GZ)
    want = (((((xh * GX + xl) * ZG + zg) * GZ + zm) * CORES) + core) * run + r
    onehot = jnp.where(src == want, 1.0, 0.0).astype(BF16)
    width = virt // MEMBERS
    for i in range(blocks):
        v = t_ref[i]
        hi = v.astype(BF16)
        rest = v - hi.astype(F32)
        mid = rest.astype(BF16)
        low = (rest - mid.astype(F32)).astype(BF16)
        parts = jnp.dot(
            jnp.concatenate([hi, mid, low], axis=0), onehot, preferred_element_type=F32
        )
        moved = (parts[:rows] + parts[rows : 2 * rows]) + parts[2 * rows :]
        for m in range(MEMBERS):
            piece = moved[:, m * width : (m + 1) * width]
            for z in range(ZL):
                out_ref[z * MEMBERS + m, :, i * width : (i + 1) * width] = piece


def regroup(t, core):
    blocks, ks, cs, virt = t.shape
    rows = ks * cs
    return pl.pallas_call(
        regroup_kernel,
        in_specs=[pl.BlockSpec(memory_space=pltpu.SMEM), pl.BlockSpec(memory_space=pltpu.VMEM)],
        out_shape=jax.ShapeDtypeStruct((ZL * MEMBERS, rows, blocks * virt // MEMBERS), F32),
        cost_estimate=pl.CostEstimate(flops=6 * blocks * rows * virt * virt, bytes_accessed=t.size * 8, transcendentals=0),
    )(core.reshape(1), t.reshape(blocks, rows, virt))


def arrange_kernel(pairs, wb, w_ref, out_ref, mid_ref, onehot_ref):
    ks = LANES // pairs
    cs = w_ref.shape[0] // wb
    wide = pairs * wb

    @pl.when(pl.program_id(0) == 0)
    def _():
        src = lax.broadcasted_iota(jnp.int32, (wide, wide), 0)
        dst = lax.broadcasted_iota(jnp.int32, (wide, wide), 1)
        onehot_ref[...] = jnp.where(src == dst % wb * pairs + dst // wb, 1.0, 0.0).astype(BF16)

    run = lax.broadcasted_iota(jnp.int32, (cs, LANES), 1) // pairs
    for h in range(wb // ks):
        tiles = [w_ref[pl.ds(h * ks + n, cs, stride=wb), :] for n in range(ks)]
        d = 1
        while d < ks:
            low = run // d % 2 == 0
            for n in range(ks):
                if n // d % 2 == 0:
                    a, b = tiles[n], tiles[n + d]
                    tiles[n] = jnp.where(low, a, pltpu.roll(b, d * pairs, 1))
                    tiles[n + d] = jnp.where(low, pltpu.roll(a, LANES - d * pairs, 1), b)
            d *= 2
        for n in range(ks):
            mid_ref[n * cs : (n + 1) * cs, h * LANES : (h + 1) * LANES] = tiles[n]
    v = mid_ref[...]
    hi = v.astype(BF16)
    rest = v - hi.astype(F32)
    mid = rest.astype(BF16)
    low = (rest - mid.astype(F32)).astype(BF16)
    n = v.shape[0]
    got = jnp.dot(jnp.concatenate([hi, mid, low], axis=0), onehot_ref[...], preferred_element_type=F32)
    out_ref[...] = ((got[:n] + got[n : 2 * n]) + got[2 * n :]).reshape(out_ref.shape)


def arrange(w, occupied, rows_of):
    cs, wb, kj = w.shape
    pairs = kj // occupied
    blocks = occupied * cs // rows_of
    steps = kj // LANES
    return pl.pallas_call(
        functools.partial(arrange_kernel, pairs, wb),
        grid=(steps,),
        in_specs=[pl.BlockSpec((cs * wb, LANES), lambda g: (0, g))],
        out_specs=pl.BlockSpec((blocks // steps, rows_of, pairs * wb), lambda g: (g, 0, 0)),
        out_shape=jax.ShapeDtypeStruct((blocks, rows_of, pairs * wb), F32),
        scratch_shapes=[
            pltpu.VMEM((LANES // pairs * cs, pairs * wb), F32),
            pltpu.VMEM((pairs * wb, pairs * wb), BF16),
        ],
        cost_estimate=pl.CostEstimate(
            flops=6 * occupied * cs * (pairs * wb) ** 2, bytes_accessed=8 * w.size, transcendentals=0
        ),
    )(w.reshape(cs * wb, kj))


def multiply_kernel(has_acc, blocks, picks, n_t, n_w, *refs):
    s_ref = refs[0]
    t_refs = refs[1 : 1 + n_t]
    w_refs = refs[1 + n_t : 1 + n_t + n_w]
    accs = refs[1 + n_t + n_w : -CORES]
    outs = refs[-CORES:]
    left = jnp.concatenate(
        [t[z, s_ref[SLOTS + n]] for t in t_refs for z in range(t.shape[0]) for n in picks], axis=0
    )
    right = jnp.concatenate([w[0] for w in w_refs], axis=0)
    lh, ll = split2(left)
    rh, rl = split2(right)
    total = lax.dot_general(
        jnp.concatenate([lh, lh, ll], axis=0),
        jnp.concatenate([rh, rl, rh], axis=0),
        (((0,), (0,)), ((), ())),
        preferred_element_type=F32,
    )
    run = total.shape[0] // (blocks * CORES * PEERS)
    total = total.reshape(blocks, CORES, PEERS, run, total.shape[1])
    for i in range(blocks):
        rows = slice(i * run, (i + 1) * run)
        for c in range(CORES):
            if has_acc:
                outs[c][:, rows, :] = accs[c][:, rows, :] + total[i, c]
            else:
                outs[c][:, rows, :] = total[i, c]


def multiply(scalars, at, ts, ws, picks, acc, blocks):
    ws = [ws[n] for n in picks]
    rows, width = ts[0].shape[2], ts[0].shape[3]
    wide = ws[0].shape[2]
    out_shape = (PEERS, width // (CORES * PEERS), wide)
    slots = [sum(COUNTS[:n]) + m for n in at for m in range(COUNTS[n])]
    in_specs = [pl.BlockSpec(t.shape, lambda z, s: (0, 0, 0, 0)) for t in ts]
    in_specs += [
        pl.BlockSpec((1, rows, wide), lambda z, s, slot=slot: (s[slot], 0, 0)) for slot in slots for _ in ws
    ]
    args = [scalars, *ts, *(list(ws) * len(slots))]
    whole = pl.BlockSpec(out_shape, lambda z, s: (0, 0, 0))
    if acc is not None:
        in_specs += [whole] * CORES
        args += acc
    depth = len(slots) * len(ws) * rows
    return pl.pallas_call(
        functools.partial(multiply_kernel, acc is not None, blocks, picks, len(ts), len(slots) * len(ws)),
        grid_spec=pltpu.PrefetchScalarGridSpec(num_scalar_prefetch=1, grid=(1,), in_specs=in_specs, out_specs=[whole] * CORES),
        out_shape=[jax.ShapeDtypeStruct(out_shape, F32)] * CORES,
        compiler_params=pltpu.CompilerParams(vmem_limit_bytes=32 * 2**20),
        cost_estimate=pl.CostEstimate(
            flops=6 * depth * width * wide, bytes_accessed=4 * depth * (width + wide), transcendentals=0
        ),
    )(*args)


def shards(t_pair, w_ovov):
    blocks, ks, cs, virt = t_pair.shape
    rows = ks * cs
    row, col = lax.axis_index("row"), lax.axis_index("col")
    scalars = jnp.concatenate(
        [
            lax.dynamic_index_in_dim(jnp.asarray(row_table()), row, keepdims=False),
            lax.dynamic_index_in_dim(jnp.asarray(col_table()), col, keepdims=False),
        ]
    )

    sent = regroup(t_pair, (col % CORES).astype(jnp.int32))
    own = lax.all_to_all(
        sent, ("row", "col"), 0, 0, tiled=True, axis_index_groups=MEMBER_GROUPS
    ).reshape(ZL, MEMBERS, rows, -1)

    depth, wb, kj = w_ovov.shape
    occupied = ks * ZL * Y
    pairs = kj // occupied
    own_w = arrange(w_ovov, occupied, rows)
    own, own_w = lax.optimization_barrier((own, own_w))
    swap_core = col_perm(lambda x, zh, c: (x, zh, c ^ 1))
    swap_x = col_perm(lambda x, zh, c: (x ^ 1, zh, c))
    swap_z = col_perm(lambda x, zh, c: (x, zh ^ 1, c))

    meets = [[row_perm(lambda z, q, f=f: (z, f(q))) for f in pair] for pair in MEETS]
    halves = [own[:1], own[1:]]
    got = [(own,)]
    near = {(0, 0): own_w}
    raw = lax.ppermute(w_ovov, "col", swap_z)
    for step in range(1, Y // 2 + 1):
        moved = [lax.ppermute(h, "row", meets[n][(step + 1) % 2]) for n, h in enumerate(halves)]
        if step == 1:
            *moved, held = lax.optimization_barrier((*moved, own_w))
            near[1, 0] = lax.ppermute(held, "col", swap_x)
        if step == HOLD:
            *moved, raw = lax.optimization_barrier((*moved, raw))
            near[0, 1] = arrange(raw, occupied, rows)
            near[1, 1] = lax.ppermute(near[0, 1], "col", swap_x)
        if step == 1:
            got[0] += tuple(moved)
            halves = [jnp.concatenate([h, m]) for h, m in zip(halves, moved)]
        else:
            got.append(tuple(moved))
            halves = moved
    ws = [near[key] for key in FROM]

    acc = None
    for at, picks in PLAN:
        ts = [t for n in at for t in got[n]]
        acc = multiply(scalars, at, ts, ws, picks, acc, blocks)

    acc = acc[0] + lax.ppermute(acc[1], "col", swap_core)
    arrived = lax.all_to_all(acc, "col", 0, 0, tiled=True, axis_index_groups=PEER_GROUPS)
    total = jnp.sum(arrived, axis=0)
    run = virt // (X * ZH * CORES)
    return total.reshape(blocks, run, pairs, wb).transpose(1, 0, 2, 3)


def solution(mesh):
    return jax.shard_map(
        shards,
        mesh=mesh,
        in_specs=(P(None, "row", "col", None), P("col", "row", None)),
        out_specs=P("col", None, None, "row"),
        check_vma=False,
    )
```

```python
import functools

import jax
import jax.numpy as jnp
import numpy as np
from jax import lax
from jax.experimental import pallas as pl
from jax.experimental.pallas import tpu as pltpu
from jax.sharding import PartitionSpec as P

X, ZH, CORES = 8, 4, 2
ZL, Y = 2, 8
GX = 2
XH = X // GX
MEMBERS = GX * CORES
PEERS = XH * ZH
LANES = 128
F32 = jnp.float32
BF16 = jnp.bfloat16


def col_of(x, zh, core):
    return (x * ZH + zh) * CORES + core


def col_perm(move):
    pairs = []
    for x in range(X):
        for zh in range(ZH):
            for core in range(CORES):
                pairs.append((col_of(x, zh, core), col_of(*move(x, zh, core))))
    return pairs


def row_perm(move):
    pairs = []
    for zl in range(ZL):
        for y in range(Y):
            z2, y2 = move(zl, y)
            pairs.append((zl * Y + y, z2 * Y + y2 % Y))
    return pairs


MEMBER_GROUPS = [
    [
        (zl * Y + y) * (X * ZH * CORES) + col_of(xh * GX + xl, zh, core)
        for zl in range(ZL)
        for xl in range(GX)
        for core in range(CORES)
    ]
    for y in range(Y)
    for xh in range(XH)
    for zh in range(ZH)
]
PEER_GROUPS = [
    [col_of(xh * GX + xl, zh, core) for xh in range(XH) for zh in range(ZH)]
    for xl in range(GX)
    for core in range(CORES)
]


def low_pair(y):
    return y ^ 1


def high_pair(y):
    return (y + 1 if y % 2 else y - 1) % Y


MEETS = [(low_pair, high_pair), (high_pair, low_pair)]


def sources(y):
    per_half = []
    for first, second in MEETS:
        steps = [[lambda q: q], [first]]
        held = steps[0] + steps[1]
        for n in range(2, Y // 2 + 1):
            meet = second if n % 2 == 0 else first
            held = [lambda q, f=f, meet=meet: f(meet(q)) for f in held]
            steps.append(held)
        per_half.append([[f(y) for f in step] for step in steps])
    zero, one = per_half
    calls = [[(0, y), (1, y)] + [(0, q) for q in zero[1]] + [(1, q) for q in one[1]]]
    for n in range(2, Y // 2 + 1):
        calls.append([(0, q) for q in zero[n]] + [(1, q) for q in one[n]])
    return calls


COUNTS = [len(call) for call in sources(0)]
SLOTS = sum(COUNTS)


def row_table():
    table = np.zeros((ZL * Y, SLOTS), np.int32)
    for row in range(ZL * Y):
        table[row] = [zl * Y + q for call in sources(row % Y) for zl, q in call]
    return table


def col_table():
    table = np.zeros((X * ZH * CORES, MEMBERS), np.int32)
    for col in range(table.shape[0]):
        x, core = col // (ZH * CORES), col % CORES
        for n in range(MEMBERS):
            source = (x - n % GX) % GX
            table[col, n] = source * CORES + (core if n < GX else 1 - core)
    return table


def split2(v):
    hi = v.astype(BF16)
    return hi, (v - hi.astype(F32)).astype(BF16)


def regroup_kernel(t_ref, out_ref):
    blocks, rows, virt = t_ref.shape[0], t_ref.shape[1], t_ref.shape[2]
    run = virt // (X * ZH * CORES)
    src = lax.broadcasted_iota(jnp.int32, (virt, virt), 0)
    dst = lax.broadcasted_iota(jnp.int32, (virt, virt), 1)
    r = dst % run
    zh = (dst // run) % ZH
    xh = (dst // (run * ZH)) % XH
    core = (dst // (run * ZH * XH)) % CORES
    xl = dst // (run * ZH * XH * CORES)
    want = ((((xh * GX + xl) * ZH + zh) * CORES) + core) * run + r
    onehot = jnp.where(src == want, 1.0, 0.0).astype(BF16)
    width = virt // MEMBERS
    for i in range(blocks):
        v = t_ref[i]
        hi = v.astype(BF16)
        rest = v - hi.astype(F32)
        mid = rest.astype(BF16)
        low = (rest - mid.astype(F32)).astype(BF16)
        parts = jnp.dot(
            jnp.concatenate([hi, mid, low], axis=0), onehot, preferred_element_type=F32
        )
        moved = (parts[:rows] + parts[rows : 2 * rows]) + parts[2 * rows :]
        for m in range(MEMBERS):
            piece = moved[:, m * width : (m + 1) * width]
            for z in range(ZL):
                out_ref[z * MEMBERS + m, :, i * width : (i + 1) * width] = piece


def regroup(t):
    blocks, ks, cs, virt = t.shape
    rows = ks * cs
    return pl.pallas_call(
        regroup_kernel,
        out_shape=jax.ShapeDtypeStruct((ZL * MEMBERS, rows, blocks * virt // MEMBERS), F32),
        cost_estimate=pl.CostEstimate(flops=6 * blocks * rows * virt * virt, bytes_accessed=t.size * 8, transcendentals=0),
    )(t.reshape(blocks, rows, virt))


def arrange_kernel(pairs, wb, w_ref, out_ref, mid_ref, onehot_ref):
    ks = LANES // pairs
    cs = w_ref.shape[0] // wb
    wide = pairs * wb

    @pl.when(pl.program_id(0) == 0)
    def _():
        src = lax.broadcasted_iota(jnp.int32, (wide, wide), 0)
        dst = lax.broadcasted_iota(jnp.int32, (wide, wide), 1)
        onehot_ref[...] = jnp.where(src == dst % wb * pairs + dst // wb, 1.0, 0.0).astype(BF16)

    run = lax.broadcasted_iota(jnp.int32, (cs, LANES), 1) // pairs
    for h in range(wb // ks):
        tiles = [w_ref[pl.ds(h * ks + n, cs, stride=wb), :] for n in range(ks)]
        d = 1
        while d < ks:
            low = run // d % 2 == 0
            for n in range(ks):
                if n // d % 2 == 0:
                    a, b = tiles[n], tiles[n + d]
                    tiles[n] = jnp.where(low, a, pltpu.roll(b, d * pairs, 1))
                    tiles[n + d] = jnp.where(low, pltpu.roll(a, LANES - d * pairs, 1), b)
            d *= 2
        for n in range(ks):
            mid_ref[n * cs : (n + 1) * cs, h * LANES : (h + 1) * LANES] = tiles[n]
    v = mid_ref[...]
    hi = v.astype(BF16)
    rest = v - hi.astype(F32)
    mid = rest.astype(BF16)
    low = (rest - mid.astype(F32)).astype(BF16)
    n = v.shape[0]
    got = jnp.dot(jnp.concatenate([hi, mid, low], axis=0), onehot_ref[...], preferred_element_type=F32)
    out_ref[...] = ((got[:n] + got[n : 2 * n]) + got[2 * n :]).reshape(out_ref.shape)


def arrange(w, occupied, rows_of):
    cs, wb, kj = w.shape
    pairs = kj // occupied
    blocks = occupied * cs // rows_of
    steps = kj // LANES
    return pl.pallas_call(
        functools.partial(arrange_kernel, pairs, wb),
        grid=(steps,),
        in_specs=[pl.BlockSpec((cs * wb, LANES), lambda g: (0, g))],
        out_specs=pl.BlockSpec((blocks // steps, rows_of, pairs * wb), lambda g: (g, 0, 0)),
        out_shape=jax.ShapeDtypeStruct((blocks, rows_of, pairs * wb), F32),
        scratch_shapes=[
            pltpu.VMEM((LANES // pairs * cs, pairs * wb), F32),
            pltpu.VMEM((pairs * wb, pairs * wb), BF16),
        ],
        cost_estimate=pl.CostEstimate(
            flops=6 * occupied * cs * (pairs * wb) ** 2, bytes_accessed=8 * w.size, transcendentals=0
        ),
    )(w.reshape(cs * wb, kj))


def multiply_kernel(has_acc, blocks, order_at, n_t, n_w, *refs):
    s_ref = refs[0]
    t_refs = refs[1 : 1 + n_t]
    w_refs = refs[1 + n_t : 1 + n_t + n_w]
    out_ref = refs[-1]
    left = jnp.concatenate(
        [t[z, s_ref[order_at + n]] for t in t_refs for z in range(t.shape[0]) for n in range(MEMBERS)], axis=0
    )
    right = jnp.concatenate([w[0] for w in w_refs], axis=0)
    lh, ll = split2(left)
    rh, rl = split2(right)
    total = lax.dot_general(
        jnp.concatenate([lh, lh, ll], axis=0),
        jnp.concatenate([rh, rl, rh], axis=0),
        (((0,), (0,)), ((), ())),
        preferred_element_type=F32,
    )
    run = total.shape[0] // (blocks * PEERS)
    total = total.reshape(blocks, PEERS, run, total.shape[1])
    for i in range(blocks):
        rows = slice(i * run, (i + 1) * run)
        if has_acc:
            out_ref[:, rows, :] = refs[1 + n_t + n_w][:, rows, :] + total[i]
        else:
            out_ref[:, rows, :] = total[i]


def multiply(scalars, at, ts, ws, acc, blocks):
    rows, width = ts[0].shape[2], ts[0].shape[3]
    wide = ws[0].shape[2]
    out_shape = (PEERS, width // PEERS, wide)
    first = sum(COUNTS[:at])
    slots = range(first, first + COUNTS[at])
    in_specs = [pl.BlockSpec(t.shape, lambda z, s: (0, 0, 0, 0)) for t in ts]
    in_specs += [
        pl.BlockSpec((1, rows, wide), lambda z, s, slot=slot: (s[slot], 0, 0)) for slot in slots for _ in ws
    ]
    args = [scalars, *ts, *(list(ws) * len(slots))]
    whole = pl.BlockSpec(out_shape, lambda z, s: (0, 0, 0))
    if acc is not None:
        in_specs.append(whole)
        args.append(acc)
    depth = len(slots) * len(ws) * rows
    return pl.pallas_call(
        functools.partial(multiply_kernel, acc is not None, blocks, SLOTS, len(ts), len(slots) * len(ws)),
        grid_spec=pltpu.PrefetchScalarGridSpec(num_scalar_prefetch=1, grid=(1,), in_specs=in_specs, out_specs=whole),
        out_shape=jax.ShapeDtypeStruct(out_shape, F32),
        compiler_params=pltpu.CompilerParams(vmem_limit_bytes=32 * 2**20),
        cost_estimate=pl.CostEstimate(
            flops=6 * depth * width * wide, bytes_accessed=4 * depth * (width + wide), transcendentals=0
        ),
    )(*args)


def shards(t_pair, w_ovov):
    blocks, ks, cs, virt = t_pair.shape
    rows = ks * cs
    row, col = lax.axis_index("row"), lax.axis_index("col")
    scalars = jnp.concatenate(
        [
            lax.dynamic_index_in_dim(jnp.asarray(row_table()), row, keepdims=False),
            lax.dynamic_index_in_dim(jnp.asarray(col_table()), col, keepdims=False),
        ]
    )

    sent = regroup(t_pair)
    own = lax.all_to_all(
        sent, ("row", "col"), 0, 0, tiled=True, axis_index_groups=MEMBER_GROUPS
    ).reshape(ZL, MEMBERS, rows, -1)

    depth, wb, kj = w_ovov.shape
    occupied = ks * ZL * Y
    pairs = kj // occupied
    own_w = arrange(w_ovov, occupied, rows)
    swap_core = col_perm(lambda x, zh, c: (x, zh, 1 - c))
    swap_x = col_perm(lambda x, zh, c: (x ^ 1, zh, c))
    w_x = lax.ppermute(own_w, "col", swap_x)
    w_c = lax.ppermute(own_w, "col", swap_core)

    meets = [[row_perm(lambda z, q, f=f: (z, f(q))) for f in pair] for pair in MEETS]
    halves = [own[:1], own[1:]]
    got = [(own,)]
    for step in range(1, Y // 2 + 1):
        moved = [lax.ppermute(h, "row", meets[n][(step + 1) % 2]) for n, h in enumerate(halves)]
        if step == 1:
            got[0] += tuple(moved)
            halves = [jnp.concatenate([h, m]) for h, m in zip(halves, moved)]
        else:
            got.append(tuple(moved))
            halves = moved
        if step == 1:
            w_x, _ = lax.optimization_barrier((w_x, halves[1]))
    w_xc = lax.ppermute(w_x, "col", swap_core)
    ws = [own_w, w_x, w_c, w_xc]

    acc = None
    for at, ts in enumerate(got):
        acc = multiply(scalars, at, ts, ws, acc, blocks)

    arrived = lax.all_to_all(acc, "col", 0, 0, tiled=True, axis_index_groups=PEER_GROUPS)
    total = jnp.sum(arrived, axis=0)
    run = virt // (X * ZH * CORES)
    return total.reshape(blocks, run, pairs, wb).transpose(1, 0, 2, 3)


def solution(mesh):
    return jax.shard_map(
        shards,
        mesh=mesh,
        in_specs=(P(None, "row", "col", None), P("col", "row", None)),
        out_specs=P("col", None, None, "row"),
        check_vma=False,
    )
```

```python
import functools

import jax
import jax.numpy as jnp
import numpy as np
from jax import lax
from jax.experimental import pallas as pl
from jax.experimental.pallas import tpu as pltpu
from jax.sharding import PartitionSpec as P

X, ZH, CORES = 8, 4, 2
ZL, Y = 2, 8
GX = 2
XH = X // GX
MEMBERS = GX * CORES
PEERS = XH * ZH
LANES = 128
F32 = jnp.float32
BF16 = jnp.bfloat16


def col_of(x, zh, core):
    return (x * ZH + zh) * CORES + core


def col_perm(move):
    pairs = []
    for x in range(X):
        for zh in range(ZH):
            for core in range(CORES):
                pairs.append((col_of(x, zh, core), col_of(*move(x, zh, core))))
    return pairs


def row_perm(move):
    pairs = []
    for zl in range(ZL):
        for y in range(Y):
            z2, y2 = move(zl, y)
            pairs.append((zl * Y + y, z2 * Y + y2 % Y))
    return pairs


MEMBER_GROUPS = [
    [
        (zl * Y + y) * (X * ZH * CORES) + col_of(xh * GX + xl, zh, core)
        for zl in range(ZL)
        for xl in range(GX)
        for core in range(CORES)
    ]
    for y in range(Y)
    for xh in range(XH)
    for zh in range(ZH)
]
PEER_GROUPS = [
    [col_of(xh * GX + xl, zh, core) for xh in range(XH) for zh in range(ZH)]
    for xl in range(GX)
    for core in range(CORES)
]


def low_pair(y):
    return y ^ 1


def high_pair(y):
    return (y + 1 if y % 2 else y - 1) % Y


MEETS = [(low_pair, high_pair), (high_pair, low_pair)]


def sources(y):
    per_half = []
    for first, second in MEETS:
        steps = [[lambda q: q], [first]]
        held = steps[0] + steps[1]
        for n in range(2, Y // 2 + 1):
            meet = second if n % 2 == 0 else first
            held = [lambda q, f=f, meet=meet: f(meet(q)) for f in held]
            steps.append(held)
        per_half.append([[f(y) for f in step] for step in steps])
    zero, one = per_half
    calls = [[(0, y), (1, y)] + [(0, q) for q in zero[1]] + [(1, q) for q in one[1]]]
    for n in range(2, Y // 2 + 1):
        calls.append([(0, q) for q in zero[n]] + [(1, q) for q in one[n]])
    return calls


COUNTS = [len(call) for call in sources(0)]
SLOTS = sum(COUNTS)


def row_table():
    table = np.zeros((ZL * Y, SLOTS), np.int32)
    for row in range(ZL * Y):
        table[row] = [zl * Y + q for call in sources(row % Y) for zl, q in call]
    return table


def col_table():
    table = np.zeros((X * ZH * CORES, MEMBERS), np.int32)
    for col in range(table.shape[0]):
        x, core = col // (ZH * CORES), col % CORES
        for n in range(MEMBERS):
            source = (x - n % GX) % GX
            table[col, n] = source * CORES + (core if n < GX else 1 - core)
    return table


def split2(v):
    hi = v.astype(BF16)
    return hi, (v - hi.astype(F32)).astype(BF16)


def regroup_kernel(t_ref, out_ref):
    blocks, rows, virt = t_ref.shape[0], t_ref.shape[1], t_ref.shape[2]
    run = virt // (X * ZH * CORES)
    src = lax.broadcasted_iota(jnp.int32, (virt, virt), 0)
    dst = lax.broadcasted_iota(jnp.int32, (virt, virt), 1)
    r = dst % run
    zh = (dst // run) % ZH
    xh = (dst // (run * ZH)) % XH
    core = (dst // (run * ZH * XH)) % CORES
    xl = dst // (run * ZH * XH * CORES)
    want = ((((xh * GX + xl) * ZH + zh) * CORES) + core) * run + r
    onehot = jnp.where(src == want, 1.0, 0.0).astype(BF16)
    width = virt // MEMBERS
    for i in range(blocks):
        v = t_ref[i]
        hi = v.astype(BF16)
        rest = v - hi.astype(F32)
        mid = rest.astype(BF16)
        low = (rest - mid.astype(F32)).astype(BF16)
        parts = jnp.dot(
            jnp.concatenate([hi, mid, low], axis=0), onehot, preferred_element_type=F32
        )
        moved = (parts[:rows] + parts[rows : 2 * rows]) + parts[2 * rows :]
        for m in range(MEMBERS):
            piece = moved[:, m * width : (m + 1) * width]
            for z in range(ZL):
                out_ref[z * MEMBERS + m, :, i * width : (i + 1) * width] = piece


def regroup(t):
    blocks, ks, cs, virt = t.shape
    rows = ks * cs
    return pl.pallas_call(
        regroup_kernel,
        out_shape=jax.ShapeDtypeStruct((ZL * MEMBERS, rows, blocks * virt // MEMBERS), F32),
        cost_estimate=pl.CostEstimate(flops=6 * blocks * rows * virt * virt, bytes_accessed=t.size * 8, transcendentals=0),
    )(t.reshape(blocks, rows, virt))


def arrange_kernel(pairs, wb, w_ref, out_ref, mid_ref, onehot_ref):
    ks = LANES // pairs
    cs = w_ref.shape[0] // wb
    wide = pairs * wb

    @pl.when(pl.program_id(0) == 0)
    def _():
        src = lax.broadcasted_iota(jnp.int32, (wide, wide), 0)
        dst = lax.broadcasted_iota(jnp.int32, (wide, wide), 1)
        onehot_ref[...] = jnp.where(src == dst % wb * pairs + dst // wb, 1.0, 0.0).astype(BF16)

    run = lax.broadcasted_iota(jnp.int32, (cs, LANES), 1) // pairs
    for h in range(wb // ks):
        tiles = [w_ref[pl.ds(h * ks + n, cs, stride=wb), :] for n in range(ks)]
        d = 1
        while d < ks:
            low = run // d % 2 == 0
            for n in range(ks):
                if n // d % 2 == 0:
                    a, b = tiles[n], tiles[n + d]
                    tiles[n] = jnp.where(low, a, pltpu.roll(b, d * pairs, 1))
                    tiles[n + d] = jnp.where(low, pltpu.roll(a, LANES - d * pairs, 1), b)
            d *= 2
        for n in range(ks):
            mid_ref[n * cs : (n + 1) * cs, h * LANES : (h + 1) * LANES] = tiles[n]
    v = mid_ref[...]
    hi = v.astype(BF16)
    rest = v - hi.astype(F32)
    mid = rest.astype(BF16)
    low = (rest - mid.astype(F32)).astype(BF16)
    n = v.shape[0]
    got = jnp.dot(jnp.concatenate([hi, mid, low], axis=0), onehot_ref[...], preferred_element_type=F32)
    out_ref[...] = ((got[:n] + got[n : 2 * n]) + got[2 * n :]).reshape(out_ref.shape)


def arrange(w, occupied, rows_of):
    cs, wb, kj = w.shape
    pairs = kj // occupied
    blocks = occupied * cs // rows_of
    steps = kj // LANES
    return pl.pallas_call(
        functools.partial(arrange_kernel, pairs, wb),
        grid=(steps,),
        in_specs=[pl.BlockSpec((cs * wb, LANES), lambda g: (0, g))],
        out_specs=pl.BlockSpec((blocks // steps, rows_of, pairs * wb), lambda g: (g, 0, 0)),
        out_shape=jax.ShapeDtypeStruct((blocks, rows_of, pairs * wb), F32),
        scratch_shapes=[
            pltpu.VMEM((LANES // pairs * cs, pairs * wb), F32),
            pltpu.VMEM((pairs * wb, pairs * wb), BF16),
        ],
        cost_estimate=pl.CostEstimate(
            flops=6 * occupied * cs * (pairs * wb) ** 2, bytes_accessed=8 * w.size, transcendentals=0
        ),
    )(w.reshape(cs * wb, kj))


def multiply_kernel(has_acc, blocks, order_at, n_t, n_w, *refs):
    s_ref = refs[0]
    t_refs = refs[1 : 1 + n_t]
    w_refs = refs[1 + n_t : 1 + n_t + n_w]
    out_ref = refs[-1]
    left = jnp.concatenate(
        [t[z, s_ref[order_at + n]] for t in t_refs for z in range(t.shape[0]) for n in range(MEMBERS)], axis=0
    )
    right = jnp.concatenate([w[0] for w in w_refs], axis=0)
    lh, ll = split2(left)
    rh, rl = split2(right)
    total = lax.dot_general(
        jnp.concatenate([lh, lh, ll], axis=0),
        jnp.concatenate([rh, rl, rh], axis=0),
        (((0,), (0,)), ((), ())),
        preferred_element_type=F32,
    )
    run = total.shape[0] // (blocks * PEERS)
    total = total.reshape(blocks, PEERS, run, total.shape[1])
    for i in range(blocks):
        rows = slice(i * run, (i + 1) * run)
        if has_acc:
            out_ref[:, rows, :] = refs[1 + n_t + n_w][:, rows, :] + total[i]
        else:
            out_ref[:, rows, :] = total[i]


def multiply(scalars, at, ts, ws, acc, blocks):
    rows, width = ts[0].shape[2], ts[0].shape[3]
    wide = ws[0].shape[2]
    out_shape = (PEERS, width // PEERS, wide)
    first = sum(COUNTS[:at])
    slots = range(first, first + COUNTS[at])
    in_specs = [pl.BlockSpec(t.shape, lambda z, s: (0, 0, 0, 0)) for t in ts]
    in_specs += [
        pl.BlockSpec((1, rows, wide), lambda z, s, slot=slot: (s[slot], 0, 0)) for slot in slots for _ in ws
    ]
    args = [scalars, *ts, *(list(ws) * len(slots))]
    whole = pl.BlockSpec(out_shape, lambda z, s: (0, 0, 0))
    if acc is not None:
        in_specs.append(whole)
        args.append(acc)
    depth = len(slots) * len(ws) * rows
    return pl.pallas_call(
        functools.partial(multiply_kernel, acc is not None, blocks, SLOTS, len(ts), len(slots) * len(ws)),
        grid_spec=pltpu.PrefetchScalarGridSpec(num_scalar_prefetch=1, grid=(1,), in_specs=in_specs, out_specs=whole),
        out_shape=jax.ShapeDtypeStruct(out_shape, F32),
        compiler_params=pltpu.CompilerParams(vmem_limit_bytes=32 * 2**20),
        cost_estimate=pl.CostEstimate(
            flops=6 * depth * width * wide, bytes_accessed=4 * depth * (width + wide), transcendentals=0
        ),
    )(*args)


def shards(t_pair, w_ovov):
    blocks, ks, cs, virt = t_pair.shape
    rows = ks * cs
    row, col = lax.axis_index("row"), lax.axis_index("col")
    scalars = jnp.concatenate(
        [
            lax.dynamic_index_in_dim(jnp.asarray(row_table()), row, keepdims=False),
            lax.dynamic_index_in_dim(jnp.asarray(col_table()), col, keepdims=False),
        ]
    )

    sent = regroup(t_pair)
    own = lax.all_to_all(
        sent, ("row", "col"), 0, 0, tiled=True, axis_index_groups=MEMBER_GROUPS
    ).reshape(ZL, MEMBERS, rows, -1)

    depth, wb, kj = w_ovov.shape
    occupied = ks * ZL * Y
    pairs = kj // occupied
    own_w = arrange(w_ovov, occupied, rows)
    swap_core = col_perm(lambda x, zh, c: (x, zh, 1 - c))
    swap_x = col_perm(lambda x, zh, c: (x ^ 1, zh, c))
    w_x = lax.ppermute(own_w, "col", swap_x)

    meets = [[row_perm(lambda z, q, f=f: (z, f(q))) for f in pair] for pair in MEETS]
    halves = [own[:1], own[1:]]
    got = [(own,)]
    for step in range(1, Y // 2 + 1):
        moved = [lax.ppermute(h, "row", meets[n][(step + 1) % 2]) for n, h in enumerate(halves)]
        if step == 1:
            got[0] += tuple(moved)
            halves = [jnp.concatenate([h, m]) for h, m in zip(halves, moved)]
        else:
            got.append(tuple(moved))
            halves = moved
        if step == 1:
            *halves, held_w = lax.optimization_barrier((*halves, own_w))
            w_c = lax.ppermute(held_w, "col", swap_core)
        if step == 2:
            *halves, w_x = lax.optimization_barrier((*halves, w_x))
            got[-1] = tuple(halves)
            w_xc = lax.ppermute(w_x, "col", swap_core)
            ws = [own_w, w_x, w_c, w_xc]
        if step == 3:
            acc = multiply(scalars, 0, got[0], ws, None, blocks)
            *halves, acc = lax.optimization_barrier((*halves, acc))
            got[-1] = tuple(halves)

    for at, ts in enumerate(got[1:], 1):
        acc = multiply(scalars, at, ts, ws, acc, blocks)

    arrived = lax.all_to_all(acc, "col", 0, 0, tiled=True, axis_index_groups=PEER_GROUPS)
    total = jnp.sum(arrived, axis=0)
    run = virt // (X * ZH * CORES)
    return total.reshape(blocks, run, pairs, wb).transpose(1, 0, 2, 3)


def solution(mesh):
    return jax.shard_map(
        shards,
        mesh=mesh,
        in_specs=(P(None, "row", "col", None), P("col", "row", None)),
        out_specs=P("col", None, None, "row"),
        check_vma=False,
    )
```
